128 devices in a mesh: row: 4 (over z_hi, core), col: 32 (over x, y, z_lo).
Axes of the slice: x: 4, y: 4, z: 4 (z_hi: 2, z_lo: 2; z = z_hi * 2 + z_lo), core: 2. Of those that a mesh axis runs over, the one named last changes fastest.
Arguments:
- homolog_embedding: bfloat16 [256, 1024, 256], P('col', 'row'), may hold values from -6 to 6
- pairwise: bfloat16 [1024, 1024, 128], P('row', 'col'), may hold values from -6 to 6
- alignment_mask: int32 [256, 1024], P('col', 'row'), may hold values 0 or 1
- residue_mask: int32 [1024], replicated, may hold values 0 or 1
- query_key_value_gate_matrix: bfloat16 [256, 1024], replicated, may hold values from -0.375 to 0.375
- attend_exit_matrix: bfloat16 [256, 256], replicated, may hold values from -0.375 to 0.375
- bias_weight: float32 [128, 8], replicated, may hold values from -30 to 30
- widen_matrix: bfloat16 [256, 1024], replicated, may hold values from -0.375 to 0.375
- shrink_matrix: bfloat16 [1024, 256], replicated, may hold values from -0.1875 to 0.1875
- left_right_matrix: bfloat16 [256, 64], replicated, may hold values from -0.375 to 0.375
- outer_weight: bfloat16 [1024, 128], replicated, may hold values from -2 to 2
Outputs:
- new_alignment: bfloat16 [256, 1024, 256], P('col', 'row')
- new_pairwise: bfloat16 [1024, 1024, 128], P('row', 'col')
The draws below stay inside these ranges and needn't reach their ends.
All inputs are finite; a program needn't handle non-finite values. No bound on the sum of `alignment_mask` on one device may be relied on, other than what follows from the above.
Results may differ from the reference program's by a relative error of at most 0.018.
Values may be sent and summed in bfloat16 or wider, within the bound.
A program may use at most 128 MiB of HBM per device.

```python
import jax
import jax.numpy as jnp
from jax import lax

EMBED_BREADTH = 256
C_Z = 128
ATTEND_GROUPS = 8
GROUP_BREADTH = 32
OUTER_SIDE_WIDTH = 32
MIDDLE_UNITS = 1024
HOMOLOG_NUMBER = 256
CROP_POSITIONS = 1024
N_ROW = 4


def draw_bias_weight(key, part):
    key = jax.random.fold_in(key, 11)
    base = jax.random.truncated_normal(key, -4.0, 4.0, (C_Z, ATTEND_GROUPS), jnp.float32)
    spread = 1.5 * jnp.ones((ATTEND_GROUPS,), jnp.float32)
    return jnp.clip(base * spread[None, :] / C_Z ** 0.5, -30.0, 30.0)


def plant(values, rng, least, largest):
    dims = values.shape
    index_at = [jax.random.randint(jax.random.fold_in(rng, axis), (), 0, dims[axis]) for axis in range(len(dims))]
    values = values.at[tuple(index_at)].set(least)
    longest = dims.index(max(dims))
    index_at[longest] = (index_at[longest] + 1) % dims[longest]
    return values.at[tuple(index_at)].set(largest)


def steps_of(rng, dims, shards, least, high):
    def one(position, blocks):
        heights = jax.random.uniform(jax.random.fold_in(jax.random.fold_in(rng, 6), position), (blocks,), jnp.float32, least / len(shards), high / len(shards))
        return jnp.repeat(jnp.exp(heights), dims[position] // blocks).reshape((-1,) + (1,) * (len(dims) - position - 1))

    level = one(*shards[0])
    for cut in shards[1:]:
        level = level * one(*cut)
    return level


def noise(rng, shape, scale, bound, split=(), kind=jnp.bfloat16):
    loudness = steps_of(rng, shape, split, -0.22, 0.18) if split else 1.0
    entries = jax.random.normal(rng, shape, jnp.float32) * scale * loudness
    return jnp.minimum(jnp.maximum(entries, -bound), bound).astype(kind)


def setup_inputs(seed: int = 0) -> dict:
    streams_of = jax.random.split(jax.random.key(seed), 12)
    return {
        "homolog_embedding": noise(streams_of[0], (HOMOLOG_NUMBER, CROP_POSITIONS, EMBED_BREADTH), 1.0, 6.0, ((0, 32), (1, 4))),
        "pairwise": noise(streams_of[1], (CROP_POSITIONS, CROP_POSITIONS, C_Z), 1.0, 6.0, ((0, 4), (1, 32))),
        "alignment_mask": plant((jax.random.randint(streams_of[2], (HOMOLOG_NUMBER, CROP_POSITIONS), 0, 4) < 3).astype(jnp.int32), jax.random.fold_in(streams_of[2], 1), 0, 1),
        "residue_mask": plant((jax.random.randint(streams_of[3], (CROP_POSITIONS,), 0, 8) < 7).astype(jnp.int32), jax.random.fold_in(streams_of[3], 1), 0, 1),
        "query_key_value_gate_matrix": noise(streams_of[4], (EMBED_BREADTH, 4 * ATTEND_GROUPS * GROUP_BREADTH), EMBED_BREADTH ** -0.5, 0.375),
        "attend_exit_matrix": noise(streams_of[5], (ATTEND_GROUPS * GROUP_BREADTH, EMBED_BREADTH), (ATTEND_GROUPS * GROUP_BREADTH) ** -0.5, 0.375),
        "bias_weight": draw_bias_weight(jax.random.fold_in(streams_of[11], 71), 0),
        "widen_matrix": noise(streams_of[7], (EMBED_BREADTH, MIDDLE_UNITS), EMBED_BREADTH ** -0.5, 0.375),
        "shrink_matrix": noise(streams_of[8], (MIDDLE_UNITS, EMBED_BREADTH), MIDDLE_UNITS ** -0.5, 0.1875),
        "left_right_matrix": noise(streams_of[9], (EMBED_BREADTH, 2 * OUTER_SIDE_WIDTH), EMBED_BREADTH ** -0.5, 0.375),
        "outer_weight": noise(streams_of[10], (OUTER_SIDE_WIDTH * OUTER_SIDE_WIDTH, C_Z), 8 ** -0.5, 2.0),
    }


epsilon = 1e-05
masked_score = 1000000000.0
count_offset = 0.001

def standardize_entries(values):
    centre = lax.optimization_barrier(jnp.mean(values, -1, keepdims=True))
    centred = values - centre
    return centred * lax.rsqrt(lax.optimization_barrier(jnp.mean(centred * centred, -1, keepdims=True)) + epsilon)

def reference(homolog_embedding, pairwise, alignment_mask, residue_mask, query_key_value_gate_matrix, attend_exit_matrix, bias_weight, widen_matrix, shrink_matrix, left_right_matrix, outer_weight):
    middle_breadth = ATTEND_GROUPS * GROUP_BREADTH
    mask_float = alignment_mask.astype(jnp.float32)
    pair_normed = standardize_entries(pairwise.astype(jnp.float32))
    pair_bias = jnp.einsum('ijc,ch->hij', pair_normed, bias_weight, precision=lax.Precision.HIGHEST)
    standardized_embedding = standardize_entries(homolog_embedding.astype(jnp.float32)).astype(jnp.bfloat16)
    mapped_homologs = jnp.dot(standardized_embedding.reshape(HOMOLOG_NUMBER * CROP_POSITIONS, EMBED_BREADTH), query_key_value_gate_matrix, preferred_element_type=jnp.float32)
    mapped_homologs = mapped_homologs.reshape(HOMOLOG_NUMBER, CROP_POSITIONS, 4, middle_breadth)
    queries = (mapped_homologs[:, :, 0] * GROUP_BREADTH ** (-0.5)).astype(jnp.bfloat16)
    key_rows = mapped_homologs[:, :, 1].astype(jnp.bfloat16)
    value_rows = mapped_homologs[:, :, 2].astype(jnp.bfloat16)
    gating = jax.nn.sigmoid(mapped_homologs[:, :, 3])

    def attend(pieces):
        query_row, key_row, value_row, mask_row = pieces
        query_heads = query_row.reshape(CROP_POSITIONS, ATTEND_GROUPS, GROUP_BREADTH).astype(jnp.float32)
        key_heads = key_row.reshape(CROP_POSITIONS, ATTEND_GROUPS, GROUP_BREADTH).astype(jnp.float32)
        value_heads = value_row.reshape(CROP_POSITIONS, ATTEND_GROUPS, GROUP_BREADTH).astype(jnp.float32)
        scores = jnp.einsum('ihd,jhd->hij', query_heads, key_heads) + pair_bias
        scores = scores + ((mask_row - 1.0) * masked_score)[None, None, :]
        probs = jax.nn.softmax(scores, axis=-1).astype(jnp.bfloat16)
        attended = jnp.einsum('hij,jhd->ihd', probs.astype(jnp.float32), value_heads)
        return attended.reshape(CROP_POSITIONS, middle_breadth)
    attended = lax.map(attend, (queries, key_rows, value_rows, mask_float))
    sigmoid_scaled = (attended * gating).astype(jnp.bfloat16)
    post_attend_state = homolog_embedding.astype(jnp.float32) + jnp.dot(sigmoid_scaled.reshape(HOMOLOG_NUMBER * CROP_POSITIONS, middle_breadth), attend_exit_matrix, preferred_element_type=jnp.float32).reshape(HOMOLOG_NUMBER, CROP_POSITIONS, EMBED_BREADTH)
    perceptron_input = standardize_entries(post_attend_state).astype(jnp.bfloat16).reshape(HOMOLOG_NUMBER * CROP_POSITIONS, EMBED_BREADTH)
    middle_activations = jax.nn.relu(jnp.dot(perceptron_input, widen_matrix, preferred_element_type=jnp.float32)).astype(jnp.bfloat16)
    post_perceptron_state = post_attend_state + jnp.dot(middle_activations, shrink_matrix, preferred_element_type=jnp.float32).reshape(HOMOLOG_NUMBER, CROP_POSITIONS, EMBED_BREADTH)
    new_alignment = post_perceptron_state.astype(jnp.bfloat16)
    outer_input = standardize_entries(post_perceptron_state).astype(jnp.bfloat16).reshape(HOMOLOG_NUMBER * CROP_POSITIONS, EMBED_BREADTH)
    sides = jnp.dot(outer_input, left_right_matrix, preferred_element_type=jnp.float32).reshape(HOMOLOG_NUMBER, CROP_POSITIONS, 2, OUTER_SIDE_WIDTH)
    sides = (sides * mask_float[:, :, None, None]).astype(jnp.bfloat16)
    left_side = sides[:, :, 0]
    right_side = sides[:, :, 1].astype(jnp.float32)
    pair_count = jnp.dot(mask_float.T, mask_float, precision=lax.Precision.HIGHEST) + count_offset
    residue_float = residue_mask.astype(jnp.float32)
    pair_gate = residue_float[:, None] * residue_float[None, :]
    block_count = N_ROW * 8
    block_rows = CROP_POSITIONS // block_count
    left_blocks = left_side.reshape(HOMOLOG_NUMBER, block_count, block_rows, OUTER_SIDE_WIDTH).transpose(1, 0, 2, 3)

    def outer_block(pieces):
        left_piece, pair_piece, count_piece, gate_piece = pieces
        outer = jnp.einsum('sia,sjb->ijab', left_piece.astype(jnp.float32), right_side)
        outer = outer.reshape(block_rows * CROP_POSITIONS, OUTER_SIDE_WIDTH * OUTER_SIDE_WIDTH).astype(jnp.bfloat16)
        update = jnp.dot(outer, outer_weight, preferred_element_type=jnp.float32).reshape(block_rows, CROP_POSITIONS, C_Z)
        update = update / count_piece[:, :, None]
        return (pair_piece.astype(jnp.float32) + gate_piece[:, :, None] * update).astype(jnp.bfloat16)
    new_pairwise = lax.map(outer_block, (left_blocks, pairwise.reshape(block_count, block_rows, CROP_POSITIONS, C_Z), pair_count.reshape(block_count, block_rows, CROP_POSITIONS), pair_gate.reshape(block_count, block_rows, CROP_POSITIONS)))
    return (new_alignment, new_pairwise.reshape(CROP_POSITIONS, CROP_POSITIONS, C_Z))
```

```python
import functools

import jax
import jax.numpy as jnp
from jax import lax
from jax.experimental import pallas as pl
from jax.experimental.pallas import tpu as pltpu
from jax.sharding import PartitionSpec as P

MESH = pl.DeviceIdType.MESH
F32 = jnp.float32
BF16 = jnp.bfloat16
EPS = 1e-05
LOG2E = 1.4426950408889634
MASKED = 1000000000.0
COUNT_OFFSET = 0.001
HEADS = 8
NT = (((1,), (1,)), ((), ()))
VMEM_BYTES = 60 * 2**20


def layer_norm(v):
    d = v - jnp.mean(v, -1, keepdims=True)
    return d * lax.rsqrt(jnp.mean(d * d, -1, keepdims=True) + EPS)


class Place:
    def __init__(self):
        self.r = lax.axis_index("row")
        self.c = lax.axis_index("col")
        self.zh, self.core = self.r // 2, lax.rem(self.r, 2)
        self.x, self.y = self.c // 8, lax.rem(self.c // 2, 4)
        self.zl = lax.rem(self.c, 2)
        self.xp, self.xm = lax.rem(self.x + 1, 4), lax.rem(self.x + 3, 4)
        self.yp, self.ym = lax.rem(self.y + 1, 4), lax.rem(self.y + 3, 4)

    def at(self, zh=None, core=None, x=None, y=None, zl=None):
        zh = self.zh if zh is None else zh
        core = self.core if core is None else core
        x = self.x if x is None else x
        y = self.y if y is None else y
        zl = self.zl if zl is None else zl
        return (zh * 2 + core, (x * 4 + y) * 2 + zl)


class Sender:
    def __init__(self, send_sems, recv_sems):
        self.send_sems, self.recv_sems, self.copies = send_sems, recv_sems, []

    def start(self, src, dst, device):
        n = len(self.copies)
        copy = pltpu.make_async_remote_copy(
            src_ref=src,
            dst_ref=dst,
            send_sem=self.send_sems.at[n],
            recv_sem=self.recv_sems.at[n],
            device_id=device,
            device_id_type=MESH,
        )
        copy.start()
        self.copies.append(copy)
        return copy

    def wait_sent(self):
        for copy in self.copies:
            copy.wait_send()


class PlaneGather:
    def __init__(self, place, sender, view, x_first):
        self.p, self.s, self.view, self.x_first = place, sender, view, x_first
        self.pending = ()

    def _both(self, plus, minus, along_x):
        p = self.p
        up = p.at(x=p.xp) if along_x else p.at(y=p.yp)
        down = p.at(x=p.xm) if along_x else p.at(y=p.ym)
        self.pending = (self.s.start(plus, plus, up), self.s.start(minus, minus, down))

    def _wait(self):
        for copy in self.pending:
            copy.wait_recv()

    def first(self):
        p = self.p
        own = self.view(p.x, p.y, None)
        self._both(own, own, self.x_first)

    def first_forward(self):
        p = self.p
        self._wait()
        if self.x_first:
            self._both(self.view(p.xm, p.y, 0), self.view(p.xp, p.y, 1), True)
        else:
            self._both(self.view(p.x, p.ym, 0), self.view(p.x, p.yp, 1), False)

    def second(self):
        p = self.p
        self._wait()
        every = slice(0, 4)
        line = self.view(every, p.y, None) if self.x_first else self.view(p.x, every, None)
        self._both(line, line, not self.x_first)

    def second_forward(self):
        p = self.p
        self._wait()
        low, high = slice(0, 2), slice(2, 4)
        if self.x_first:
            self._both(self.view(low, p.ym, None), self.view(high, p.yp, None), False)
        else:
            self._both(self.view(p.xm, low, None), self.view(p.xp, high, None), True)

    def finish(self):
        self._wait()


def window(index):
    return pl.ds(index.start, index.stop - index.start) if isinstance(index, slice) else index


def greet(devices):
    barrier = pltpu.get_barrier_semaphore()
    for device in devices:
        pl.semaphore_signal(barrier, inc=1, device_id=device, device_id_type=MESH)
    return barrier


def fold_max(v):
    parts = [v[8 * i : 8 * i + 8] for i in range(v.shape[0] // 8)]
    while len(parts) > 1:
        parts = [
            jnp.maximum(parts[i], parts[i + 1]) if i + 1 < len(parts) else parts[i]
            for i in range(0, len(parts), 2)
        ]
    return parts[0]


def attention_kernel(
    x_ref, pair_ref, mask_ref, w_ref, bw_ref,
    out_ref,
    pair32, stage, bias, xg, maskg, maskb, kt, vt, qt, gate, att,
    s0, s1, s2, s3, send_sems, recv_sems,
):
    p = Place()
    peers = (
        p.at(x=p.xp), p.at(x=p.xm), p.at(y=p.yp), p.at(y=p.ym),
        p.at(zl=1 - p.zl), p.at(core=1 - p.core), p.at(zh=1 - p.zh),
    )
    barrier = greet(peers)
    sender = Sender(send_sems, recv_sems)

    pair32[...] = pair_ref[...].astype(F32)
    bw = jnp.transpose(bw_ref[...]) * LOG2E
    bw_high = bw.astype(BF16)
    bw_low = (bw - bw_high.astype(F32)).astype(BF16)
    bw_rows = jnp.concatenate([bw_high, bw_low], 0)
    bw_both = jnp.concatenate([bw_rows, bw_rows], 1)

    @pl.loop(0, 8)
    def _(jb):
        for u in range(4):
            j = jb * 4 + u
            n = layer_norm(pair32[pl.ds(j, 256, stride=32), :])
            high = n.astype(BF16)
            low = (n - high.astype(F32)).astype(BF16)
            both = jnp.concatenate([high, low], 1)
            r = lax.dot_general(bw_both, both, NT, preferred_element_type=F32)
            r = r[:8] + r[8:]
            for t in range(2):
                stage[t, pl.ds(j, 8, stride=32), :] = r[:, t * 128 : t * 128 + 128]

    for h in range(HEADS):
        rows = slice(h * 32, h * 32 + 32)
        bias[h, p.x, p.y, pl.ds(p.zl * 32, 32), :] = jnp.concatenate([stage[0, rows, :], stage[1, rows, :]], 1)
    pl.semaphore_wait(barrier, len(peers))

    z_copies = []
    for h in range(HEADS):
        own = bias.at[h, p.x, p.y, pl.ds(p.zl * 32, 32)]
        z_copies.append(sender.start(own, own, p.at(zl=1 - p.zl)))

    for s in range(8):
        xg[s, p.r] = layer_norm(x_ref[s].astype(F32)).astype(BF16)
    maskg[p.r] = (mask_ref[...].astype(F32) - 1.0) * (MASKED * LOG2E)
    core_peer, z_peer = p.at(core=1 - p.core), p.at(zh=1 - p.zh)
    far = (1 - p.zh) * 2 + p.core
    mask_copies = [
        sender.start(maskg.at[p.r], maskg.at[p.r], core_peer),
        sender.start(maskg.at[p.r], maskg.at[p.r], z_peer),
    ]
    near_copies, far_copies, pass_copies = [], [], []
    for g in range(4):
        own = xg.at[pl.ds(2 * g, 2), p.r]
        far_copies.append(sender.start(own, own, z_peer))
        near_copies.append(sender.start(own, own, core_peer))

    def head_view(h):
        def view(x, y, half):
            if half is None:
                return bias.at[h, window(x), window(y)]
            return bias.at[h, x, y, pl.ds(half * 32, 32)]

        return view

    gathers = [PlaneGather(p, sender, head_view(h), h % 2 == 0) for h in range(HEADS)]

    def advance(slot):
        for k in range(4):
            stage = slot - k
            for h in (2 * k, 2 * k + 1):
                if stage == 0:
                    z_copies[h].wait_recv()
                    gathers[h].first()
                elif stage == 1:
                    gathers[h].first_forward()
                elif stage == 2:
                    gathers[h].second()
                elif stage == 3:
                    gathers[h].second_forward()
                elif stage == 4:
                    gathers[h].finish()

    advance(0)

    wq = w_ref[:, 0:256]
    wk = w_ref[:, 256:512]
    wv = w_ref[:, 512:768]
    wg = w_ref[:, 768:1024]
    wq_t = jnp.transpose(wq.astype(F32)).astype(BF16)
    wv_t = jnp.transpose(wv.astype(F32)).astype(BF16)
    for s in range(8):
        own = xg[s, p.r]
        q = lax.dot_general(wq_t, own, NT, preferred_element_type=F32)
        qt[s] = (q * (LOG2E * 32**-0.5)).astype(BF16)
        gate[s] = jax.nn.sigmoid(jnp.dot(own, wg, preferred_element_type=F32))
        if s == 1:
            advance(1)
        if s == 5:
            advance(2)

    for copy in mask_copies:
        copy.wait_recv()
    mask_copies.append(sender.start(maskg.at[far], maskg.at[far], core_peer))
    for g in range(4):
        far_copies[g].wait_recv()
        piece = xg.at[pl.ds(2 * g, 2), far]
        pass_copies.append(sender.start(piece, piece, core_peer))
        if g == 1:
            advance(3)
    mask_copies[2].wait_recv()
    for r in range(4):
        columns = jnp.transpose(maskg[r])
        for s in range(8):
            maskb[s, r * 256 : r * 256 + 256, :] = jnp.broadcast_to(columns[:, s : s + 1], (256, 128))

    vt[:, :, 32:48, :] = jnp.ones((8, 8, 16, 1024), BF16)
    for g in range(4):
        near_copies[g].wait_recv()
        pass_copies[g].wait_recv()

        @pl.loop(2 * g, 2 * g + 2)
        def _(s):
            for r in range(4):
                rows = xg[s, r]
                k = jnp.dot(rows, wk, preferred_element_type=F32).astype(BF16)
                kt[s, 0, r * 256 : r * 256 + 256, :] = k[:, :128]
                kt[s, 1, r * 256 : r * 256 + 256, :] = k[:, 128:]
                v = lax.dot_general(wv_t, rows, NT, preferred_element_type=F32).astype(BF16)
                vt[s, :, 0:32, r * 256 : r * 256 + 256] = v.reshape(8, 32, 256)

    head_of = lax.broadcasted_iota(jnp.int32, (128, 256), 0) // 32

    def step(new, new_scores, now, now_scores, now_max):
        new_max, total = [None, None], [None, None]
        if new is not None:
            h, first = new
            tile = h // 4
            q = [
                jnp.where(
                    head_of == h % 4, qt[first + u, tile * 128 : tile * 128 + 128, :].astype(F32), 0.0
                ).astype(BF16)
                for u in range(2)
            ]
        for jc in range(4):
            rows = slice(jc * 256, jc * 256 + 256)
            if new is not None:
                b = bias[h, jc].reshape(256, 256)
                for u in range(2):
                    m = maskb[first + u, rows, :]
                    sc = jnp.dot(kt[first + u, tile, rows, :], q[u], preferred_element_type=F32)
                    sc = sc + b + jnp.concatenate([m, m], 1)
                    new_scores[u][rows, :] = sc
                    f = fold_max(sc)
                    new_max[u] = f if new_max[u] is None else jnp.maximum(new_max[u], f)
            if now is not None:
                hn, start = now
                for u in range(2):
                    e = jnp.exp2(now_scores[u][rows, :] - now_max[u]).astype(BF16)
                    a = jnp.dot(vt[start + u, hn, :, rows], e, preferred_element_type=F32)
                    total[u] = a if total[u] is None else total[u] + a
        if now is not None:
            for u in range(2):
                att[start + u, hn * 32 : hn * 32 + 32, :] = total[u][:32] / total[u][32:33]
        if new is not None:
            return tuple(jnp.max(m, axis=0, keepdims=True) for m in new_max)

    even, odd = (s0, s1), (s2, s3)
    advance(4)
    top = None
    for k in range(4):
        for h in (2 * k, 2 * k + 1):
            top = step((h, 0), even, None, None, None)
            top = step((h, 2), odd, (h, 0), even, top)
            top = step((h, 4), even, (h, 2), odd, top)
            top = step((h, 6), odd, (h, 4), even, top)
            step(None, None, (h, 6), odd, top)
        if k < 3:
            advance(5 + k)

    for s in range(8):
        out_ref[s] = (jnp.transpose(att[s]) * gate[s]).astype(BF16)
    sender.wait_sent()


def transition_kernel(
    x_ref, gated_ref, pair_ref, mask_ref, res_ref, wo_ref, w1_ref, w2_ref, wlr_ref, ow_ref,
    align_ref, out_ref,
    lscr, rscr, zsend, zrecv, zmask, zmask_in, left, maskall, rsend, rrecv, rt, obuf, acc, upd, counts, col_scr,
    send_sems, recv_sems, r_send_sems, r_recv_sems,
):
    p = Place()
    home = p.c // 8
    barrier = greet((p.at(x=p.xp), p.at(x=p.xm), p.at(y=p.yp), p.at(y=p.ym), p.at(zl=1 - p.zl)))

    @pl.loop(0, 32)
    def _(c):
        @pl.when(jnp.logical_or(home != p.r, c != p.c))
        def _():
            pl.semaphore_signal(barrier, inc=1, device_id=(home, c), device_id_type=MESH)

    sender = Sender(send_sems, recv_sems)
    mask = mask_ref[...].astype(F32)

    wl = wlr_ref[:, 0:32].astype(F32)
    wr = wlr_ref[:, 32:64]
    wl_t = jnp.transpose(wl).astype(BF16)
    wr4 = jnp.concatenate([wr, wr, wr, wr], 1)
    mask_cols = jnp.transpose(mask)

    for g in range(4):
        rows = x_ref[2 * g : 2 * g + 2].reshape(512, 256).astype(F32)
        gated = gated_ref[2 * g : 2 * g + 2].reshape(512, 256)
        after = rows + jnp.dot(gated, wo_ref[...], preferred_element_type=F32)
        hidden = jnp.dot(layer_norm(after).astype(BF16), w1_ref[...], preferred_element_type=F32)
        hidden = jnp.maximum(hidden, 0.0).astype(BF16)
        after = after + jnp.dot(hidden, w2_ref[...], preferred_element_type=F32)
        align_ref[2 * g : 2 * g + 2] = after.astype(BF16).reshape(2, 256, 256)
        n = layer_norm(after).astype(BF16)
        l = lax.dot_general(wl_t, n, NT, preferred_element_type=F32)
        rr = jnp.dot(n, wr4, preferred_element_type=F32)
        for u in range(2):
            s = 2 * g + u
            masked = l[:, u * 256 : u * 256 + 256] * mask[s : s + 1, :]
            for t in range(2):
                lscr[t, s * 32 : s * 32 + 32, :] = masked[:, t * 128 : t * 128 + 128]
            rscr[s * 256 : s * 256 + 256, :] = rr[u * 256 : u * 256 + 256] * mask_cols[:, s : s + 1]

    pl.semaphore_wait(barrier, 5 + 32 - (home == p.r).astype(jnp.int32))

    z_peer = p.at(zl=1 - p.zl)
    own_left = [
        jnp.concatenate([lscr[t, pl.ds(a, 8, stride=32), :] for t in range(2)], 1) for a in range(32)
    ]
    for g in range(4):
        for q in range(4):
            both = jnp.concatenate([own_left[8 * g + q], own_left[8 * g + 4 + q]], 0)
            zsend[g, :, q * 256 : q * 256 + 256] = both.astype(BF16)
    zmask[...] = jnp.concatenate([mask, mask], 0).astype(BF16)
    z_copies = [sender.start(zsend.at[g], zrecv.at[g], z_peer) for g in range(4)]
    z_mask = sender.start(zmask, zmask_in, z_peer)

    lane = lax.broadcasted_iota(jnp.int32, (8, 128), 1) // 32
    for k in range(8):
        halves = []
        for half in range(2):
            parts = []
            for q in range(4):
                j = k * 32 + half * 16 + q * 4
                v = [rscr[pl.ds(j + u, 8, stride=256), :] for u in range(4)]
                parts.append(jnp.where(lane == 0, v[0], jnp.where(lane == 1, v[1], jnp.where(lane == 2, v[2], v[3]))))
            tile = k // 4
            parts.append(mask[:, tile * 128 : tile * 128 + 128])
            halves.append(jnp.concatenate(parts, 1))
        rsend[k] = jnp.concatenate(halves, 0).astype(BF16)

    def right_copy(k, row):
        return pltpu.make_async_remote_copy(
            src_ref=rsend.at[k],
            dst_ref=rrecv.at[p.c],
            send_sem=r_send_sems.at[k * 4 + row],
            recv_sem=r_recv_sems.at[p.c],
            device_id=(row, p.r * 8 + k),
            device_id_type=MESH,
        )

    own_block = p.c - p.r * 8

    def is_remote(k, row):
        return jnp.logical_or(own_block != k, p.r != row)

    @pl.loop(0, 32)
    def _(n):
        k, row = n // 4, lax.rem(n, 4)

        @pl.when(is_remote(k, row))
        def _():
            right_copy(k, row).start()

        @pl.when(jnp.logical_not(is_remote(k, row)))
        def _():
            pltpu.make_async_copy(rsend.at[k], rrecv.at[p.c], r_recv_sems.at[p.c]).start()

    def left_view(g, base):
        def view(x, y, half):
            lanes = pl.ds(base, 1024) if half is None else pl.ds(base + half * 512, 512)
            return left.at[g, window(x), window(y), pl.ds(0, 16), lanes]

        return view

    def mask_view(x, y, half):
        lanes = pl.ds(0, 256) if half is None else pl.ds(half * 128, 128)
        return maskall.at[window(x), window(y), pl.ds(0, 16), lanes]

    mask_gather = PlaneGather(p, sender, mask_view, True)
    gathers = [(PlaneGather(p, sender, left_view(g, 0), True), PlaneGather(p, sender, left_view(g, 1024), False)) for g in range(4)]
    first_in_pair = p.zl == 0

    def pair_rows(own, other):
        a = jnp.where(first_in_pair, own, other)
        b = jnp.where(first_in_pair, other, own)
        return jnp.concatenate([a, b], 0).astype(BF16)

    for g in range(4):
        z_copies[g].wait_recv()
        for q in range(4):
            other = zrecv[g, :, q * 256 : q * 256 + 256].astype(F32)
            left[g, p.x, p.y, :, q * 256 : q * 256 + 256] = pair_rows(own_left[8 * g + q], other[:8])
            left[g, p.x, p.y, :, 1024 + q * 256 : 1024 + q * 256 + 256] = pair_rows(own_left[8 * g + 4 + q], other[8:])
        for unit in gathers[g]:
            unit.first()
    z_mask.wait_recv()
    maskall[p.x, p.y] = pair_rows(mask, zmask_in[...].astype(F32)[:8])
    mask_gather.first()

    def advance(slot):
        for g in range(4):
            stage = slot - g
            units = gathers[g] + ((mask_gather,) if g == 0 else ())
            for unit in units:
                if stage == 0:
                    unit.first_forward()
                elif stage == 1:
                    unit.second()
                elif stage == 2:
                    unit.second_forward()
                elif stage == 3:
                    unit.finish()

    advance(0)

    for c in range(32):
        pltpu.make_async_copy(rrecv.at[c], rrecv.at[c], r_recv_sems.at[c]).wait()
    advance(1)
    slabs = rrecv[...].astype(F32)
    for half in range(2):
        rows = slabs[:, half * 8 : half * 8 + 8, :].reshape(256, 640)
        rt[half * 512 : half * 512 + 512, :] = jnp.transpose(rows[:, :512]).astype(BF16)
        if half == 0:
            col_scr[...] = jnp.transpose(rows[:, 512:]).astype(F32)
    advance(2)

    ow_t = jnp.transpose(ow_ref[...].astype(F32)).astype(BF16)
    place_in_tile = pl.multiple_of(lax.rem(p.c, 4) * 32, 32)
    advance(3)
    mask_j = col_scr[pl.ds(place_in_tile, 32), :].astype(BF16)
    mask_i = maskall[...].reshape(256, 256)
    pair_count = jnp.dot(mask_j, mask_i, preferred_element_type=F32) + COUNT_OFFSET
    res = res_ref[...].astype(F32)
    rowid = lax.broadcasted_iota(jnp.int32, (8, 128), 0)
    pick = lambda n: jnp.sum(jnp.where(rowid == n, res, 0.0), 0, keepdims=True)
    res_i = jnp.concatenate([pick(p.r * 2), pick(p.r * 2 + 1)], 1)
    res_j = jnp.transpose(jnp.broadcast_to(pick(p.c // 4), (128, 128)))
    col_scr[:, 0:128] = res_j
    res_j = col_scr[pl.ds(place_in_tile, 32), 0:128]
    counts[...] = jnp.concatenate([res_j, res_j], 1) * res_i / pair_count

    for g in range(4):

        @pl.loop(0, 8)
        def _(a):
            l = left[g, :, :, :, pl.ds(pl.multiple_of(a * 256, 256), 256)].reshape(256, 256)
            o = jnp.dot(rt[...], l, preferred_element_type=F32).astype(BF16)
            obuf[:, a] = o.reshape(32, 32, 256)

        wt = ow_t[:, g * 256 : g * 256 + 256]

        @pl.loop(0, 16)
        def _(jb):
            for u in range(2):
                j = jb * 2 + u
                o = jnp.dot(wt, obuf[j].reshape(256, 256), preferred_element_type=F32)
                if g > 0:
                    o = o + acc[j]
                if g < 3:
                    acc[j] = o
                else:
                    o = o * counts[pl.ds(j, 1), :]
                    upd[pl.ds(j, 256, stride=32), :] = jnp.transpose(o)

        if g < 3:
            advance(4 + g)

    @pl.loop(0, 8)
    def _(n):
        rows = pl.ds(pl.multiple_of(n * 1024, 1024), 1024)
        out_ref[rows, :] = (pair_ref[rows, :].astype(F32) + upd[rows, :]).astype(BF16)

    sender.wait_sent()

    @pl.loop(0, 32)
    def _(n):
        k, row = n // 4, lax.rem(n, 4)

        @pl.when(is_remote(k, row))
        def _():
            right_copy(k, row).wait_send()


def vmem(n):
    return [pl.BlockSpec(memory_space=pltpu.VMEM)] * n


def attend(x, pair, mask, w, bw):
    copies = 8 + 3 + 12 + 64
    return pl.pallas_call(
        attention_kernel,
        out_shape=jax.ShapeDtypeStruct((8, 256, 256), BF16),
        in_specs=vmem(5),
        out_specs=pl.BlockSpec(memory_space=pltpu.VMEM),
        scratch_shapes=[
            pltpu.VMEM((8192, 128), F32),
            pltpu.VMEM((2, 256, 128), F32),
            pltpu.VMEM((8, 4, 4, 64, 256), F32),
            pltpu.VMEM((8, 4, 256, 256), BF16),
            pltpu.VMEM((4, 8, 256), F32),
            pltpu.VMEM((8, 1024, 128), F32),
            pltpu.VMEM((8, 2, 1024, 128), BF16),
            pltpu.VMEM((8, 8, 48, 1024), BF16),
            pltpu.VMEM((8, 256, 256), BF16),
            pltpu.VMEM((8, 256, 256), F32),
            pltpu.VMEM((8, 256, 256), F32),
        ]
        + [pltpu.VMEM((1024, 256), F32)] * 4
        + [pltpu.SemaphoreType.DMA((copies,)), pltpu.SemaphoreType.DMA((copies,))],
        compiler_params=pltpu.CompilerParams(collective_id=0, has_side_effects=True, vmem_limit_bytes=VMEM_BYTES),
    )(x, pair, mask, w, bw)


def transition(x, gated, pair, mask, res, wo, w1, w2, wlr, ow):
    copies = 5 + 8 * 9
    return pl.pallas_call(
        transition_kernel,
        out_shape=(
            jax.ShapeDtypeStruct((8, 256, 256), BF16),
            jax.ShapeDtypeStruct((8192, 128), BF16),
        ),
        in_specs=vmem(10),
        out_specs=tuple(vmem(2)),
        scratch_shapes=[
            pltpu.VMEM((2, 256, 128), F32),
            pltpu.VMEM((2048, 128), F32),
            pltpu.VMEM((4, 16, 1024), BF16),
            pltpu.VMEM((4, 16, 1024), BF16),
            pltpu.VMEM((16, 256), BF16),
            pltpu.VMEM((16, 256), BF16),
            pltpu.VMEM((4, 4, 4, 16, 2048), BF16),
            pltpu.VMEM((4, 4, 16, 256), BF16),
            pltpu.VMEM((8, 16, 640), BF16),
            pltpu.VMEM((32, 16, 640), BF16),
            pltpu.VMEM((1024, 256), BF16),
            pltpu.VMEM((32, 8, 32, 256), BF16),
            pltpu.VMEM((32, 128, 256), F32),
            pltpu.VMEM((8192, 128), F32),
            pltpu.VMEM((32, 256), F32),
            pltpu.VMEM((128, 256), F32),
            pltpu.SemaphoreType.DMA((copies,)),
            pltpu.SemaphoreType.DMA((copies,)),
            pltpu.SemaphoreType.DMA((32,)),
            pltpu.SemaphoreType.DMA((32,)),
        ],
        compiler_params=pltpu.CompilerParams(collective_id=1, has_side_effects=True, vmem_limit_bytes=VMEM_BYTES),
    )(x, gated, pair, mask, res, wo, w1, w2, wlr, ow)


def per_device(x, pairwise, mask, residue_mask, w, wo, bw, w1, w2, wlr, ow):
    pair = pairwise.reshape(8192, 128)
    gated = attend(x, pair, mask, w, bw)
    alignment, new_pair = transition(x, gated, pair, mask, residue_mask.reshape(8, 128), wo, w1, w2, wlr, ow)
    return alignment, new_pair.reshape(256, 32, 128)


def solution(mesh):
    return jax.shard_map(
        per_device,
        mesh=mesh,
        in_specs=(P("col", "row", None), P("row", "col", None), P("col", "row")) + (P(),) * 8,
        out_specs=(P("col", "row", None), P("row", "col", None)),
        check_vma=False,
    )
```

```python
import functools

import jax
import jax.numpy as jnp
from jax import lax
from jax.experimental import pallas as pl
from jax.experimental.pallas import tpu as pltpu
from jax.sharding import PartitionSpec as P

MESH = pl.DeviceIdType.MESH
F32 = jnp.float32
BF16 = jnp.bfloat16
EPS = 1e-05
LOG2E = 1.4426950408889634
MASKED = 1000000000.0
COUNT_OFFSET = 0.001
HEADS = 8
NT = (((1,), (1,)), ((), ()))
VMEM_BYTES = 60 * 2**20


def layer_norm(v):
    d = v - jnp.mean(v, -1, keepdims=True)
    return d * lax.rsqrt(jnp.mean(d * d, -1, keepdims=True) + EPS)


class Place:
    def __init__(self):
        self.r = lax.axis_index("row")
        self.c = lax.axis_index("col")
        self.zh, self.core = self.r // 2, lax.rem(self.r, 2)
        self.x, self.y = self.c // 8, lax.rem(self.c // 2, 4)
        self.zl = lax.rem(self.c, 2)
        self.xp, self.xm = lax.rem(self.x + 1, 4), lax.rem(self.x + 3, 4)
        self.yp, self.ym = lax.rem(self.y + 1, 4), lax.rem(self.y + 3, 4)
        self.xo, self.yo = lax.rem(self.x + 2, 4), lax.rem(self.y + 2, 4)

    def along(self, on_x):
        if on_x:
            return [self.at(x=x) for x in (self.xp, self.xm, self.xo)]
        return [self.at(y=y) for y in (self.yp, self.ym, self.yo)]

    def along_with_pair(self, on_x):
        other = 1 - self.zl
        if on_x:
            return self.along(True) + [self.at(x=x, zl=other) for x in (self.x, self.xp, self.xm, self.xo)]
        return self.along(False) + [self.at(y=y, zl=other) for y in (self.y, self.yp, self.ym, self.yo)]

    def at(self, zh=None, core=None, x=None, y=None, zl=None):
        zh = self.zh if zh is None else zh
        core = self.core if core is None else core
        x = self.x if x is None else x
        y = self.y if y is None else y
        zl = self.zl if zl is None else zl
        return (zh * 2 + core, (x * 4 + y) * 2 + zl)


class Sender:
    def __init__(self, send_sems, recv_sems):
        self.send_sems, self.recv_sems, self.copies = send_sems, recv_sems, []

    def start(self, src, dst, device):
        n = len(self.copies)
        copy = pltpu.make_async_remote_copy(
            src_ref=src,
            dst_ref=dst,
            send_sem=self.send_sems.at[n],
            recv_sem=self.recv_sems.at[n],
            device_id=device,
            device_id_type=MESH,
        )
        copy.start()
        self.copies.append(copy)
        return copy

    def wait_sent(self):
        for copy in self.copies:
            copy.wait_send()


class PlaneGather:
    def __init__(self, place, sender, view, x_first):
        self.p, self.s, self.view, self.x_first = place, sender, view, x_first
        self.pending = ()

    def _ring(self, plus, minus):
        p = self.p
        up = p.at(y=p.yp) if self.x_first else p.at(x=p.xp)
        down = p.at(y=p.ym) if self.x_first else p.at(x=p.xm)
        self.pending = (self.s.start(plus, plus, up), self.s.start(minus, minus, down))

    def _wait(self):
        for copy in self.pending:
            copy.wait_recv()

    def first(self, own, devices):
        self.pending = tuple(self.s.start(own, own, device) for device in devices)

    def second(self):
        p = self.p
        self._wait()
        every = slice(0, 4)
        line = self.view(every, p.y) if self.x_first else self.view(p.x, every)
        self._ring(line, line)

    def second_forward(self):
        p = self.p
        self._wait()
        low, high = slice(0, 2), slice(2, 4)
        if self.x_first:
            self._ring(self.view(low, p.ym), self.view(high, p.yp))
        else:
            self._ring(self.view(p.xm, low), self.view(p.xp, high))

    def finish(self):
        self._wait()


def window(index):
    return pl.ds(index.start, index.stop - index.start) if isinstance(index, slice) else index


def greet(devices):
    barrier = pltpu.get_barrier_semaphore()
    for device in devices:
        pl.semaphore_signal(barrier, inc=1, device_id=device, device_id_type=MESH)
    return barrier


def fold_max(v):
    parts = [v[8 * i : 8 * i + 8] for i in range(v.shape[0] // 8)]
    while len(parts) > 1:
        parts = [
            jnp.maximum(parts[i], parts[i + 1]) if i + 1 < len(parts) else parts[i]
            for i in range(0, len(parts), 2)
        ]
    return parts[0]


def attention_kernel(
    x_ref, pair_ref, mask_ref, w_ref, bw_ref,
    out_ref,
    pair32, stage, bias, xg, maskg, maskb, kt, vt, qt, gate, att,
    s0, s1, s2, s3, send_sems, recv_sems,
):
    p = Place()
    peers = p.along(True) + p.along(False) + [p.at(zl=1 - p.zl), p.at(core=1 - p.core), p.at(zh=1 - p.zh)]
    barrier = greet(peers)
    sender = Sender(send_sems, recv_sems)

    pair32[...] = pair_ref[...].astype(F32)
    bw = bw_ref[...] * LOG2E
    bw_high = bw.astype(BF16)
    bw_low = (bw - bw_high.astype(F32)).astype(BF16)
    bw_rows = jnp.concatenate([bw_high, bw_low], 0)
    bw_both = jnp.concatenate([bw_rows, bw_rows], 1)

    @pl.loop(0, 8)
    def _(jb):
        for u in range(4):
            j = jb * 4 + u
            n = layer_norm(pair32[pl.ds(j, 256, stride=32), :])
            high = n.astype(BF16)
            low = (n - high.astype(F32)).astype(BF16)
            both = jnp.concatenate([high, low], 1)
            r = lax.dot_general(bw_both, both, NT, preferred_element_type=F32)
            r = r[:8] + r[8:]
            for t in range(2):
                stage[t, pl.ds(j, 8, stride=32), :] = r[:, t * 128 : t * 128 + 128]

    for h in range(HEADS):
        rows = slice(h * 32, h * 32 + 32)
        bias[h, p.x, p.y, pl.ds(p.zl * 32, 32), :] = jnp.concatenate([stage[0, rows, :], stage[1, rows, :]], 1)
    pl.semaphore_wait(barrier, len(peers))

    z_copies = {}

    def to_pair(k):
        for h in (2 * k, 2 * k + 1):
            own = bias.at[h, p.x, p.y, pl.ds(p.zl * 32, 32)]
            z_copies[h] = sender.start(own, own, p.at(zl=1 - p.zl))

    to_pair(0)

    def head_view(h):
        return lambda x, y: bias.at[h, window(x), window(y)]

    gathers = [PlaneGather(p, sender, head_view(h), h % 2 == 0) for h in range(HEADS)]

    def first(k):
        for h in (2 * k, 2 * k + 1):
            z_copies[h].wait_recv()
            gathers[h].first(bias.at[h, p.x, p.y], p.along(h % 2 == 0))

    def second(k):
        for h in (2 * k, 2 * k + 1):
            gathers[h].second()

    def second_forward(k):
        for h in (2 * k, 2 * k + 1):
            gathers[h].second_forward()

    def finish(k):
        for h in (2 * k, 2 * k + 1):
            gathers[h].finish()

    def normalise(s):
        xg[s, p.r] = layer_norm(x_ref[s].astype(F32)).astype(BF16)

    core_peer, z_peer = p.at(core=1 - p.core), p.at(zh=1 - p.zh)
    far = (1 - p.zh) * 2 + p.core
    near_copies, far_copies, pass_copies = [], [], []

    def share(g):
        own = xg.at[pl.ds(2 * g, 2), p.r]
        far_copies.append(sender.start(own, own, z_peer))
        near_copies.append(sender.start(own, own, core_peer))

    wq = w_ref[:, 0:256]
    wk = w_ref[:, 256:512]
    wv = w_ref[:, 512:768]
    wg = w_ref[:, 768:1024]
    wq_t = jnp.transpose(wq.astype(F32)).astype(BF16)
    wv_t = jnp.transpose(wv.astype(F32)).astype(BF16)

    def project(s):
        own = xg[s, p.r]
        q = lax.dot_general(wq_t, own, NT, preferred_element_type=F32)
        qt[s] = (q * (LOG2E * 32**-0.5)).astype(BF16)
        gate[s] = jax.nn.sigmoid(jnp.dot(own, wg, preferred_element_type=F32))

    for s in range(4):
        normalise(s)
    first(0)
    to_pair(1)
    for s in range(4, 8):
        normalise(s)
    share(0)
    maskg[p.r] = (mask_ref[...].astype(F32) - 1.0) * (MASKED * LOG2E)
    mask_copies = [
        sender.start(maskg.at[p.r], maskg.at[p.r], core_peer),
        sender.start(maskg.at[p.r], maskg.at[p.r], z_peer),
    ]
    for s in range(4):
        project(s)
    second(0)
    first(1)
    to_pair(2)
    share(1)
    for s in range(4, 8):
        project(s)
    to_pair(3)
    for copy in mask_copies:
        copy.wait_recv()
    mask_copies.append(sender.start(maskg.at[far], maskg.at[far], core_peer))
    mask_copies[2].wait_recv()
    for r in range(4):
        columns = jnp.transpose(maskg[r])
        for s in range(8):
            maskb[s, r * 256 : r * 256 + 256, :] = jnp.broadcast_to(columns[:, s : s + 1], (256, 128))

    vt[:, :, 32:48, :] = jnp.ones((8, 8, 16, 1024), BF16)
    def pass_on(g):
        far_copies[g].wait_recv()
        piece = xg.at[pl.ds(2 * g, 2), far]
        pass_copies.append(sender.start(piece, piece, core_peer))

    second_forward(0)
    second(1)
    first(2)
    pass_on(0)
    share(2)
    for g in range(4):
        if g == 2:
            second_forward(1)
            second(2)
            first(3)
        if g < 3:
            pass_on(g + 1)
        if g == 0:
            share(3)
        near_copies[g].wait_recv()
        pass_copies[g].wait_recv()

        @pl.loop(2 * g, 2 * g + 2)
        def _(s):
            for r in range(4):
                rows = xg[s, r]
                k = jnp.dot(rows, wk, preferred_element_type=F32).astype(BF16)
                kt[s, 0, r * 256 : r * 256 + 256, :] = k[:, :128]
                kt[s, 1, r * 256 : r * 256 + 256, :] = k[:, 128:]
                v = lax.dot_general(wv_t, rows, NT, preferred_element_type=F32).astype(BF16)
                vt[s, :, 0:32, r * 256 : r * 256 + 256] = v.reshape(8, 32, 256)

    head_of = lax.broadcasted_iota(jnp.int32, (128, 256), 0) // 32

    def step(new, new_scores, now, now_scores, now_max):
        new_max, total = [None, None], [None, None]
        if new is not None:
            h, first = new
            tile = h // 4
            q = [
                jnp.where(
                    head_of == h % 4, qt[first + u, tile * 128 : tile * 128 + 128, :].astype(F32), 0.0
                ).astype(BF16)
                for u in range(2)
            ]
        for jc in range(4):
            rows = slice(jc * 256, jc * 256 + 256)
            if new is not None:
                b = bias[h, jc].reshape(256, 256)
                for u in range(2):
                    m = maskb[first + u, rows, :]
                    sc = jnp.dot(kt[first + u, tile, rows, :], q[u], preferred_element_type=F32)
                    sc = sc + b + jnp.concatenate([m, m], 1)
                    new_scores[u][rows, :] = sc
                    f = fold_max(sc)
                    new_max[u] = f if new_max[u] is None else jnp.maximum(new_max[u], f)
            if now is not None:
                hn, start = now
                for u in range(2):
                    e = jnp.exp2(now_scores[u][rows, :] - now_max[u]).astype(BF16)
                    a = jnp.dot(vt[start + u, hn, :, rows], e, preferred_element_type=F32)
                    total[u] = a if total[u] is None else total[u] + a
        if now is not None:
            for u in range(2):
                att[start + u, hn * 32 : hn * 32 + 32, :] = total[u][:32] / total[u][32:33]
        if new is not None:
            return tuple(jnp.max(m, axis=0, keepdims=True) for m in new_max)

    sets = ((s0, s1), (s2, s3))
    item = lambda n: (n // 4, 2 * (n % 4))
    finish(0)
    top = step(item(0), sets[0], None, None, None)
    for n in range(1, 4 * HEADS):
        if n % 8 == 0:
            k = n // 8
            if k < 3:
                second_forward(k + 1)
            if k == 1:
                second(3)
            finish(k)
        top = step(item(n), sets[n % 2], item(n - 1), sets[(n - 1) % 2], top)
    step(None, None, item(4 * HEADS - 1), sets[1], top)

    for s in range(8):
        out_ref[s] = (jnp.transpose(att[s]) * gate[s]).astype(BF16)
    sender.wait_sent()


def transition_kernel(
    x_ref, gated_ref, pair_ref, mask_ref, res_ref, wo_ref, w1_ref, w2_ref, wlr_ref, ow_ref,
    align_ref, out_ref,
    lscr, rscr, raw, left, maskall, rsend, rrecv, rt, obuf, upd, counts, col_scr,
    send_sems, recv_sems, r_send_sems, r_recv_sems, pass_sems,
):
    p = Place()
    home = p.c // 8
    core_peer = p.at(core=1 - p.core)
    receives = lax.rem(home, 2) == p.core
    greeted = p.along_with_pair(True) + p.along_with_pair(False) + [core_peer]
    barrier = greet(greeted)

    @pl.loop(0, 32)
    def _(c):
        @pl.when(jnp.logical_and(receives, jnp.logical_or(home != p.r, c != p.c)))
        def _():
            pl.semaphore_signal(barrier, inc=1, device_id=(home, c), device_id_type=MESH)

    sender = Sender(send_sems, recv_sems)
    mask = mask_ref[...].astype(F32)

    wl_t = wlr_ref[0:32, :]
    wr = wlr_ref[32:64, :]
    wr4 = jnp.concatenate([wr, wr, wr, wr], 0)
    mask_cols = jnp.transpose(mask)

    def transition_block(t, q):
        half = slice(t * 128, t * 128 + 128)
        four = slice(4 * q, 4 * q + 4)
        rows = x_ref[four, half, :].reshape(512, 256).astype(F32)
        gated = gated_ref[four, half, :].reshape(512, 256)
        after = rows + jnp.dot(gated, wo_ref[...], preferred_element_type=F32)
        hidden = jnp.dot(layer_norm(after).astype(BF16), w1_ref[...], preferred_element_type=F32)
        hidden = jnp.maximum(hidden, 0.0).astype(BF16)
        after = after + jnp.dot(hidden, w2_ref[...], preferred_element_type=F32)
        align_ref[four, half, :] = after.astype(BF16).reshape(4, 128, 256)
        n = layer_norm(after).astype(BF16)
        l = lax.dot_general(wl_t, n, NT, preferred_element_type=F32)
        rr = lax.dot_general(n, wr4, NT, preferred_element_type=F32)
        for u in range(4):
            s = 4 * q + u
            cols = slice(u * 128, u * 128 + 128)
            lscr[t, s * 32 : s * 32 + 32, :] = l[:, cols] * mask[s : s + 1, half]
            start = s * 256 + t * 128
            rscr[start : start + 128, :] = rr[cols] * mask_cols[half, s : s + 1]

    def own_left(t, a):
        return lscr[t, pl.ds(a, 8, stride=32), :]

    def fill_left(t):
        for a in range(16):
            both = jnp.concatenate([own_left(t, a), own_left(t, a + 16)], 0)
            raw[t, p.x, p.y, p.zl, :, a * 128 : a * 128 + 128] = both.astype(BF16)

    def left_part(t, part):
        lanes = pl.ds(part * 1024, 1024)
        view = lambda x, y: raw.at[t, window(x), window(y), pl.ds(0, 2), pl.ds(0, 16), lanes]
        own = raw.at[t, p.x, p.y, p.zl, pl.ds(0, 16), lanes]
        return PlaneGather(p, sender, view, part == 0), own, p.along_with_pair(part == 0)

    def mask_view(x, y):
        return maskall.at[window(x), window(y), pl.ds(0, 2), pl.ds(0, 16)]

    mask_unit = (
        PlaneGather(p, sender, mask_view, False),
        maskall.at[p.x, p.y, p.zl, pl.ds(0, 16)],
        p.along_with_pair(False),
    )
    halves = [[left_part(0, 0), left_part(0, 1), mask_unit], [left_part(1, 0), left_part(1, 1)]]

    def first(t):
        for unit, own, devices in halves[t]:
            unit.first(own, devices)

    def second(t):
        for unit, _, _ in halves[t]:
            unit.second()

    def second_forward(t):
        for unit, _, _ in halves[t]:
            unit.second_forward()

    def finish(t):
        for unit, _, _ in halves[t]:
            unit.finish()

    lane = lax.broadcasted_iota(jnp.int32, (8, 128), 1) // 32

    def right_copy(k, zh):
        return pltpu.make_async_remote_copy(
            src_ref=rsend.at[k],
            dst_ref=rrecv.at[p.c],
            send_sem=r_send_sems.at[k * 2 + zh],
            recv_sem=r_recv_sems.at[p.c],
            device_id=(zh * 2 + p.core, p.r * 8 + k),
            device_id_type=MESH,
        )

    def is_remote(k, zh):
        return jnp.logical_or(p.c != p.r * 8 + k, p.zh != zh)

    def send_right(t):
        for k in range(4 * t, 4 * t + 4):
            rows = []
            for half in range(2):
                parts = []
                for q in range(4):
                    j = k * 32 + half * 16 + q * 4
                    v = [rscr[pl.ds(j + u, 8, stride=256), :] for u in range(4)]
                    parts.append(
                        jnp.where(lane == 0, v[0], jnp.where(lane == 1, v[1], jnp.where(lane == 2, v[2], v[3])))
                    )
                parts.append(mask[:, t * 128 : t * 128 + 128])
                rows.append(jnp.concatenate(parts, 1))
            rsend[k] = jnp.concatenate(rows, 0).astype(BF16)

        @pl.loop(0, 8)
        def _(n):
            k, zh = 4 * t + n // 2, lax.rem(n, 2)

            @pl.when(is_remote(k, zh))
            def _():
                right_copy(k, zh).start()

            @pl.when(jnp.logical_not(is_remote(k, zh)))
            def _():
                pltpu.make_async_copy(rsend.at[k], rrecv.at[p.c], r_recv_sems.at[p.c]).start()

    right_pass = pltpu.make_async_remote_copy(
        src_ref=rrecv,
        dst_ref=rrecv,
        send_sem=pass_sems.at[0],
        recv_sem=pass_sems.at[1],
        device_id=core_peer,
        device_id_type=MESH,
    )

    transition_block(0, 0)
    transition_block(0, 1)
    fill_left(0)
    maskall[p.x, p.y, p.zl] = jnp.concatenate([mask, mask], 0).astype(BF16)
    pl.semaphore_wait(barrier, len(greeted) + 16 - (home == p.r).astype(jnp.int32))
    first(0)
    send_right(0)
    transition_block(1, 0)
    transition_block(1, 1)
    fill_left(1)
    second(0)
    first(1)
    send_right(1)
    ow_t = jnp.transpose(ow_ref[...].astype(F32)).astype(BF16)
    second_forward(0)
    second(1)

    @pl.when(receives)
    def _():
        @pl.loop(0, 32)
        def _(c):
            pltpu.make_async_copy(rrecv.at[c], rrecv.at[c], r_recv_sems.at[c]).wait()

        right_pass.start()

    @pl.when(jnp.logical_not(receives))
    def _():
        right_pass.wait_recv()

    place_in_tile = pl.multiple_of(lax.rem(p.c, 4) * 32, 32)
    for half in range(2):
        rows = rrecv[:, :, :].astype(F32)[:, half * 8 : half * 8 + 8, :].reshape(256, 640)
        rt[half * 512 : half * 512 + 512, :] = jnp.transpose(rows[:, :512]).astype(BF16)
        if half == 0:
            col_scr[...] = jnp.transpose(rows[:, 512:])
    mask_j = col_scr[pl.ds(place_in_tile, 32), :].astype(BF16)
    res = res_ref[...].astype(F32)
    rowid = lax.broadcasted_iota(jnp.int32, (8, 128), 0)
    pick = lambda n: jnp.sum(jnp.where(rowid == n, res, 0.0), 0, keepdims=True)
    res_i = jnp.concatenate([pick(p.r * 2), pick(p.r * 2 + 1)], 1)
    res_j = jnp.transpose(jnp.broadcast_to(pick(p.c // 4), (128, 128)))
    col_scr[:, 0:128] = res_j
    res_j = col_scr[pl.ds(place_in_tile, 32), 0:128]

    for t in range(2):
        finish(t)
        if t == 0:
            mask_i = maskall[...].astype(F32)[:, :, :, :8, :].reshape(256, 256).astype(BF16)
            pair_count = jnp.dot(mask_j, mask_i, preferred_element_type=F32) + COUNT_OFFSET
            factor = jnp.concatenate([res_j, res_j], 1) * res_i / pair_count
            counts[0] = factor[:, :128]
            counts[1] = factor[:, 128:]

        @pl.loop(0, 16)
        def _(n):
            x, y = n // 4, lax.rem(n, 4)
            two = raw[t, x, y].astype(F32)
            rows = pl.ds(pl.multiple_of(n * 16, 16), 16)
            for part in range(2):
                both = two[:, part * 8 : part * 8 + 8, :].reshape(16, 2048)
                left[rows, part * 2048 : part * 2048 + 2048] = both.astype(BF16)

        if t == 0:
            second_forward(1)

        @pl.loop(0, 8)
        def _(n):
            for u in range(2):
                pair = n * 2 + u
                lanes = pl.ds(pl.multiple_of(pair * 256, 256), 256)
                o = jnp.dot(rt[...], left[:, lanes], preferred_element_type=F32).astype(BF16)
                for v in range(2):
                    obuf[:, pair * 2 + v] = o[:, v * 128 : v * 128 + 128].reshape(32, 32, 128)

        @pl.loop(0, 8)
        def _(n):
            for u in range(2):
                j = n * 4 + u * 2
                two = jnp.concatenate([obuf[j + v].reshape(1024, 128) for v in range(2)], 1)
                o = jnp.dot(ow_t, two, preferred_element_type=F32)
                for v in range(2):
                    scale = counts[t, pl.ds(j + v, 1), :]
                    upd[pl.ds(t * 4096 + j + v, 128, stride=32), :] = jnp.transpose(o[:, v * 128 : v * 128 + 128] * scale)

        @pl.loop(0, 4)
        def _(n):
            rows = pl.ds(pl.multiple_of(t * 4096 + n * 1024, 1024), 1024)
            out_ref[rows, :] = (pair_ref[rows, :].astype(F32) + upd[rows, :]).astype(BF16)

    sender.wait_sent()

    @pl.when(receives)
    def _():
        right_pass.wait_send()

    @pl.loop(0, 16)
    def _(n):
        k, zh = n // 2, lax.rem(n, 2)

        @pl.when(is_remote(k, zh))
        def _():
            right_copy(k, zh).wait_send()


def vmem(n):
    return [pl.BlockSpec(memory_space=pltpu.VMEM)] * n


def attend(x, pair, mask, w, bw):
    copies = 8 + 3 + 12 + 8 * 7
    return pl.pallas_call(
        attention_kernel,
        out_shape=jax.ShapeDtypeStruct((8, 256, 256), BF16),
        in_specs=vmem(5),
        out_specs=pl.BlockSpec(memory_space=pltpu.VMEM),
        scratch_shapes=[
            pltpu.VMEM((8192, 128), F32),
            pltpu.VMEM((2, 256, 128), F32),
            pltpu.VMEM((8, 4, 4, 64, 256), F32),
            pltpu.VMEM((8, 4, 256, 256), BF16),
            pltpu.VMEM((4, 8, 256), F32),
            pltpu.VMEM((8, 1024, 128), F32),
            pltpu.VMEM((8, 2, 1024, 128), BF16),
            pltpu.VMEM((8, 8, 48, 1024), BF16),
            pltpu.VMEM((8, 256, 256), BF16),
            pltpu.VMEM((8, 256, 256), F32),
            pltpu.VMEM((8, 256, 256), F32),
        ]
        + [pltpu.VMEM((1024, 256), F32)] * 4
        + [pltpu.SemaphoreType.DMA((copies,)), pltpu.SemaphoreType.DMA((copies,))],
        compiler_params=pltpu.CompilerParams(collective_id=0, has_side_effects=True, vmem_limit_bytes=VMEM_BYTES),
    )(x, pair, mask, w, bw)


def transition(x, gated, pair, mask, res, wo, w1, w2, wlr, ow):
    copies = 5 * 11
    return pl.pallas_call(
        transition_kernel,
        out_shape=(
            jax.ShapeDtypeStruct((8, 256, 256), BF16),
            jax.ShapeDtypeStruct((8192, 128), BF16),
        ),
        in_specs=vmem(10),
        out_specs=tuple(vmem(2)),
        scratch_shapes=[
            pltpu.VMEM((2, 256, 128), F32),
            pltpu.VMEM((2048, 128), F32),
            pltpu.VMEM((2, 4, 4, 2, 16, 2048), BF16),
            pltpu.VMEM((256, 4096), BF16),
            pltpu.VMEM((4, 4, 2, 16, 256), BF16),
            pltpu.VMEM((8, 16, 640), BF16),
            pltpu.VMEM((32, 16, 640), BF16),
            pltpu.VMEM((1024, 256), BF16),
            pltpu.VMEM((32, 32, 32, 128), BF16),
            pltpu.VMEM((8192, 128), F32),
            pltpu.VMEM((2, 32, 128), F32),
            pltpu.VMEM((128, 256), F32),
            pltpu.SemaphoreType.DMA((copies,)),
            pltpu.SemaphoreType.DMA((copies,)),
            pltpu.SemaphoreType.DMA((16,)),
            pltpu.SemaphoreType.DMA((32,)),
            pltpu.SemaphoreType.DMA((2,)),
        ],
        compiler_params=pltpu.CompilerParams(collective_id=1, has_side_effects=True, vmem_limit_bytes=VMEM_BYTES),
    )(x, gated, pair, mask, res, wo, w1, w2, wlr, ow)


def per_device(x, pairwise, mask, residue_mask, w, wo, bw, w1, w2, wlr, ow):
    pair = pairwise.reshape(8192, 128)
    gated = attend(x, pair, mask, w, bw.T)
    alignment, new_pair = transition(x, gated, pair, mask, residue_mask.reshape(8, 128), wo, w1, w2, wlr.T, ow)
    return alignment, new_pair.reshape(256, 32, 128)


def solution(mesh):
    return jax.shard_map(
        per_device,
        mesh=mesh,
        in_specs=(P("col", "row", None), P("row", "col", None), P("col", "row")) + (P(),) * 8,
        out_specs=(P("col", "row", None), P("row", "col", None)),
        check_vma=False,
    )
```

```python
import functools

import jax
import jax.numpy as jnp
from jax import lax
from jax.experimental import pallas as pl
from jax.experimental.pallas import tpu as pltpu
from jax.sharding import PartitionSpec as P

MESH = pl.DeviceIdType.MESH
F32 = jnp.float32
BF16 = jnp.bfloat16
EPS = 1e-05
LOG2E = 1.4426950408889634
MASKED = 1000000000.0
COUNT_OFFSET = 0.001
HEADS = 8
NT = (((1,), (1,)), ((), ()))
VMEM_BYTES = 60 * 2**20


def layer_norm(v):
    d = v - jnp.mean(v, -1, keepdims=True)
    return d * lax.rsqrt(jnp.mean(d * d, -1, keepdims=True) + EPS)


class Place:
    def __init__(self):
        self.r = lax.axis_index("row")
        self.c = lax.axis_index("col")
        self.zh, self.core = self.r // 2, lax.rem(self.r, 2)
        self.x, self.y = self.c // 8, lax.rem(self.c // 2, 4)
        self.zl = lax.rem(self.c, 2)
        self.xp, self.xm = lax.rem(self.x + 1, 4), lax.rem(self.x + 3, 4)
        self.yp, self.ym = lax.rem(self.y + 1, 4), lax.rem(self.y + 3, 4)
        self.xo, self.yo = lax.rem(self.x + 2, 4), lax.rem(self.y + 2, 4)

    def along(self, on_x):
        if on_x:
            return [self.at(x=x) for x in (self.xp, self.xm, self.xo)]
        return [self.at(y=y) for y in (self.yp, self.ym, self.yo)]

    def along_with_pair(self, on_x):
        other = 1 - self.zl
        if on_x:
            return self.along(True) + [self.at(x=x, zl=other) for x in (self.x, self.xp, self.xm, self.xo)]
        return self.along(False) + [self.at(y=y, zl=other) for y in (self.y, self.yp, self.ym, self.yo)]

    def at(self, zh=None, core=None, x=None, y=None, zl=None):
        zh = self.zh if zh is None else zh
        core = self.core if core is None else core
        x = self.x if x is None else x
        y = self.y if y is None else y
        zl = self.zl if zl is None else zl
        return (zh * 2 + core, (x * 4 + y) * 2 + zl)


class Sender:
    def __init__(self, send_sems, recv_sems):
        self.send_sems, self.recv_sems, self.copies = send_sems, recv_sems, []

    def start(self, src, dst, device):
        n = len(self.copies)
        copy = pltpu.make_async_remote_copy(
            src_ref=src,
            dst_ref=dst,
            send_sem=self.send_sems.at[n],
            recv_sem=self.recv_sems.at[n],
            device_id=device,
            device_id_type=MESH,
        )
        copy.start()
        self.copies.append(copy)
        return copy

    def wait_sent(self):
        for copy in self.copies:
            copy.wait_send()


class PlaneGather:
    def __init__(self, place, sender, view, x_first):
        self.p, self.s, self.view, self.x_first = place, sender, view, x_first
        self.pending = ()

    def _ring(self, plus, minus):
        p = self.p
        up = p.at(y=p.yp) if self.x_first else p.at(x=p.xp)
        down = p.at(y=p.ym) if self.x_first else p.at(x=p.xm)
        self.pending = (self.s.start(plus, plus, up), self.s.start(minus, minus, down))

    def _wait(self):
        for copy in self.pending:
            copy.wait_recv()

    def first(self, own, devices):
        self.pending = tuple(self.s.start(own, own, device) for device in devices)

    def second(self):
        p = self.p
        self._wait()
        every = slice(0, 4)
        line = self.view(every, p.y) if self.x_first else self.view(p.x, every)
        self._ring(line, line)

    def second_forward(self):
        p = self.p
        self._wait()
        low, high = slice(0, 2), slice(2, 4)
        if self.x_first:
            self._ring(self.view(low, p.ym), self.view(high, p.yp))
        else:
            self._ring(self.view(p.xm, low), self.view(p.xp, high))

    def finish(self):
        self._wait()


def window(index):
    return pl.ds(index.start, index.stop - index.start) if isinstance(index, slice) else index


def greet(devices):
    barrier = pltpu.get_barrier_semaphore()
    for device in devices:
        pl.semaphore_signal(barrier, inc=1, device_id=device, device_id_type=MESH)
    return barrier


def fold_max(v):
    parts = [v[8 * i : 8 * i + 8] for i in range(v.shape[0] // 8)]
    while len(parts) > 1:
        parts = [
            jnp.maximum(parts[i], parts[i + 1]) if i + 1 < len(parts) else parts[i]
            for i in range(0, len(parts), 2)
        ]
    return parts[0]


def attention_kernel(
    x_ref, pair_ref, mask_ref, w_ref, bw_ref,
    out_ref,
    pair32, stage, bias, xg, maskg, maskb, kt, vt, qt, gate, att,
    s0, s1, s2, s3, send_sems, recv_sems,
):
    p = Place()
    peers = p.along(True) + p.along(False) + [p.at(zl=1 - p.zl), p.at(core=1 - p.core), p.at(zh=1 - p.zh)]
    barrier = greet(peers)
    sender = Sender(send_sems, recv_sems)

    pair32[...] = pair_ref[...].astype(F32)
    bw = bw_ref[...] * LOG2E
    bw_high = bw.astype(BF16)
    bw_low = (bw - bw_high.astype(F32)).astype(BF16)
    bw_rows = jnp.concatenate([bw_high, bw_low], 0)
    bw_both = jnp.concatenate([bw_rows, bw_rows], 1)

    @pl.loop(0, 8)
    def _(jb):
        for u in range(4):
            j = jb * 4 + u
            n = layer_norm(pair32[pl.ds(j, 256, stride=32), :])
            high = n.astype(BF16)
            low = (n - high.astype(F32)).astype(BF16)
            both = jnp.concatenate([high, low], 1)
            r = lax.dot_general(bw_both, both, NT, preferred_element_type=F32)
            r = r[:8] + r[8:]
            for t in range(2):
                stage[t, pl.ds(j, 8, stride=32), :] = r[:, t * 128 : t * 128 + 128]

    for h in range(HEADS):
        rows = slice(h * 32, h * 32 + 32)
        bias[h, p.x, p.y, pl.ds(p.zl * 32, 32), :] = jnp.concatenate([stage[0, rows, :], stage[1, rows, :]], 1)
    pl.semaphore_wait(barrier, len(peers))

    z_copies = {}

    def to_pair(k):
        for h in (2 * k, 2 * k + 1):
            own = bias.at[h, p.x, p.y, pl.ds(p.zl * 32, 32)]
            z_copies[h] = sender.start(own, own, p.at(zl=1 - p.zl))

    to_pair(0)

    def head_view(h):
        return lambda x, y: bias.at[h, window(x), window(y)]

    gathers = [PlaneGather(p, sender, head_view(h), h % 2 == 0) for h in range(HEADS)]

    def first(k):
        for h in (2 * k, 2 * k + 1):
            z_copies[h].wait_recv()
            gathers[h].first(bias.at[h, p.x, p.y], p.along(h % 2 == 0))

    def second(k):
        for h in (2 * k, 2 * k + 1):
            gathers[h].second()

    def second_forward(k):
        for h in (2 * k, 2 * k + 1):
            gathers[h].second_forward()

    def finish(k):
        for h in (2 * k, 2 * k + 1):
            gathers[h].finish()

    def normalise(s):
        xg[s, p.r] = layer_norm(x_ref[s].astype(F32)).astype(BF16)

    core_peer, z_peer = p.at(core=1 - p.core), p.at(zh=1 - p.zh)
    far = (1 - p.zh) * 2 + p.core
    near_copies, far_copies, pass_copies = [], [], []

    def share(g):
        own = xg.at[pl.ds(2 * g, 2), p.r]
        far_copies.append(sender.start(own, own, z_peer))
        near_copies.append(sender.start(own, own, core_peer))

    wq = w_ref[:, 0:256]
    wk = w_ref[:, 256:512]
    wv = w_ref[:, 512:768]
    wg = w_ref[:, 768:1024]
    wq_t = jnp.transpose(wq.astype(F32)).astype(BF16)
    wv_t = jnp.transpose(wv.astype(F32)).astype(BF16)

    def project(s):
        own = xg[s, p.r]
        q = lax.dot_general(wq_t, own, NT, preferred_element_type=F32)
        qt[s] = (q * (LOG2E * 32**-0.5)).astype(BF16)
        gate[s] = jax.nn.sigmoid(jnp.dot(own, wg, preferred_element_type=F32))

    for s in range(4):
        normalise(s)
    first(0)
    to_pair(1)
    for s in range(4, 8):
        normalise(s)
    share(0)
    maskg[p.r] = (mask_ref[...].astype(F32) - 1.0) * (MASKED * LOG2E)
    mask_copies = [
        sender.start(maskg.at[p.r], maskg.at[p.r], core_peer),
        sender.start(maskg.at[p.r], maskg.at[p.r], z_peer),
    ]
    for s in range(4):
        project(s)
    second(0)
    first(1)
    to_pair(2)
    to_pair(3)
    share(1)
    for s in range(4, 8):
        project(s)
    first(2)
    second(1)
    for copy in mask_copies:
        copy.wait_recv()
    mask_copies.append(sender.start(maskg.at[far], maskg.at[far], core_peer))
    mask_copies[2].wait_recv()
    for r in range(4):
        columns = jnp.transpose(maskg[r])
        for s in range(8):
            maskb[s, r * 256 : r * 256 + 256, :] = jnp.broadcast_to(columns[:, s : s + 1], (256, 128))

    vt[:, :, 32:48, :] = jnp.ones((8, 8, 16, 1024), BF16)
    def pass_on(g):
        far_copies[g].wait_recv()
        piece = xg.at[pl.ds(2 * g, 2), far]
        pass_copies.append(sender.start(piece, piece, core_peer))

    second_forward(0)
    second(2)
    first(3)
    pass_on(0)
    share(2)
    for g in range(4):
        if g == 2:
            second_forward(1)
            second(3)
        if g < 3:
            pass_on(g + 1)
        if g == 0:
            share(3)
        near_copies[g].wait_recv()
        pass_copies[g].wait_recv()

        @pl.loop(2 * g, 2 * g + 2)
        def _(s):
            for r in range(4):
                rows = xg[s, r]
                k = jnp.dot(rows, wk, preferred_element_type=F32).astype(BF16)
                kt[s, 0, r * 256 : r * 256 + 256, :] = k[:, :128]
                kt[s, 1, r * 256 : r * 256 + 256, :] = k[:, 128:]
                v = lax.dot_general(wv_t, rows, NT, preferred_element_type=F32).astype(BF16)
                vt[s, :, 0:32, r * 256 : r * 256 + 256] = v.reshape(8, 32, 256)

    head_of = lax.broadcasted_iota(jnp.int32, (128, 256), 0) // 32

    def step(new, new_scores, now, now_scores, now_max):
        new_max, total = [None, None], [None, None]
        if new is not None:
            h, first = new
            tile = h // 4
            q = [
                jnp.where(
                    head_of == h % 4, qt[first + u, tile * 128 : tile * 128 + 128, :].astype(F32), 0.0
                ).astype(BF16)
                for u in range(2)
            ]
        for jc in range(4):
            rows = slice(jc * 256, jc * 256 + 256)
            if new is not None:
                b = bias[h, jc].reshape(256, 256)
                for u in range(2):
                    m = maskb[first + u, rows, :]
                    sc = jnp.dot(kt[first + u, tile, rows, :], q[u], preferred_element_type=F32)
                    sc = sc + b + jnp.concatenate([m, m], 1)
                    new_scores[u][rows, :] = sc
                    f = fold_max(sc)
                    new_max[u] = f if new_max[u] is None else jnp.maximum(new_max[u], f)
            if now is not None:
                hn, start = now
                for u in range(2):
                    e = jnp.exp2(now_scores[u][rows, :] - now_max[u]).astype(BF16)
                    a = jnp.dot(vt[start + u, hn, :, rows], e, preferred_element_type=F32)
                    total[u] = a if total[u] is None else total[u] + a
        if now is not None:
            for u in range(2):
                att[start + u, hn * 32 : hn * 32 + 32, :] = total[u][:32] / total[u][32:33]
        if new is not None:
            return tuple(jnp.max(m, axis=0, keepdims=True) for m in new_max)

    sets = ((s0, s1), (s2, s3))
    item = lambda n: (n // 4, 2 * (n % 4))
    finish(0)
    top = step(item(0), sets[0], None, None, None)
    for n in range(1, 4 * HEADS):
        if n in (4, 12):
            second_forward(2 + n // 12)
        if n % 8 == 0:
            finish(n // 8)
        top = step(item(n), sets[n % 2], item(n - 1), sets[(n - 1) % 2], top)
    step(None, None, item(4 * HEADS - 1), sets[1], top)

    for s in range(8):
        out_ref[s] = (jnp.transpose(att[s]) * gate[s]).astype(BF16)
    sender.wait_sent()


def transition_kernel(
    x_ref, gated_ref, pair_ref, mask_ref, res_ref, wo_ref, w1_ref, w2_ref, wlr_ref, ow_ref,
    align_ref, out_ref,
    lscr, rscr, raw, left, maskall, rsend, rrecv, rt, obuf, upd, counts, col_scr,
    send_sems, recv_sems, r_send_sems, r_recv_sems, pass_sems,
):
    p = Place()
    home = p.c // 8
    core_peer = p.at(core=1 - p.core)
    receives = lax.rem(home, 2) == p.core
    greeted = p.along_with_pair(True) + p.along_with_pair(False) + [core_peer]
    barrier = greet(greeted)

    @pl.loop(0, 32)
    def _(c):
        @pl.when(jnp.logical_and(receives, jnp.logical_or(home != p.r, c != p.c)))
        def _():
            pl.semaphore_signal(barrier, inc=1, device_id=(home, c), device_id_type=MESH)

    sender = Sender(send_sems, recv_sems)
    mask = mask_ref[...].astype(F32)

    wl_t = wlr_ref[0:32, :]
    wr = wlr_ref[32:64, :]
    wr4 = jnp.concatenate([wr, wr, wr, wr], 0)
    mask_cols = jnp.transpose(mask)

    def transition_block(t, q):
        half = slice(t * 128, t * 128 + 128)
        four = slice(4 * q, 4 * q + 4)
        rows = x_ref[four, half, :].reshape(512, 256).astype(F32)
        gated = gated_ref[four, half, :].reshape(512, 256)
        after = rows + jnp.dot(gated, wo_ref[...], preferred_element_type=F32)
        hidden = jnp.dot(layer_norm(after).astype(BF16), w1_ref[...], preferred_element_type=F32)
        hidden = jnp.maximum(hidden, 0.0).astype(BF16)
        after = after + jnp.dot(hidden, w2_ref[...], preferred_element_type=F32)
        align_ref[four, half, :] = after.astype(BF16).reshape(4, 128, 256)
        n = layer_norm(after).astype(BF16)
        l = lax.dot_general(wl_t, n, NT, preferred_element_type=F32)
        rr = lax.dot_general(n, wr4, NT, preferred_element_type=F32)
        for u in range(4):
            s = 4 * q + u
            cols = slice(u * 128, u * 128 + 128)
            lscr[t, s * 32 : s * 32 + 32, :] = l[:, cols] * mask[s : s + 1, half]
            start = s * 256 + t * 128
            rscr[start : start + 128, :] = rr[cols] * mask_cols[half, s : s + 1]

    def own_left(t, a):
        return lscr[t, pl.ds(a, 8, stride=32), :]

    def fill_left(t):
        for a in range(16):
            both = jnp.concatenate([own_left(t, a), own_left(t, a + 16)], 0)
            raw[t, p.x, p.y, p.zl, :, a * 128 : a * 128 + 128] = both.astype(BF16)

    def left_part(t, part):
        lanes = pl.ds(part * 1024, 1024)
        view = lambda x, y: raw.at[t, window(x), window(y), pl.ds(0, 2), pl.ds(0, 16), lanes]
        own = raw.at[t, p.x, p.y, p.zl, pl.ds(0, 16), lanes]
        return PlaneGather(p, sender, view, part == 0), own, p.along_with_pair(part == 0)

    def mask_view(x, y):
        return maskall.at[window(x), window(y), pl.ds(0, 2), pl.ds(0, 16)]

    mask_unit = (
        PlaneGather(p, sender, mask_view, False),
        maskall.at[p.x, p.y, p.zl, pl.ds(0, 16)],
        p.along_with_pair(False),
    )
    halves = [[left_part(0, 0), left_part(0, 1), mask_unit], [left_part(1, 0), left_part(1, 1)]]

    def first(t):
        for unit, own, devices in halves[t]:
            unit.first(own, devices)

    def second(t):
        for unit, _, _ in halves[t]:
            unit.second()

    def second_forward(t):
        for unit, _, _ in halves[t]:
            unit.second_forward()

    def finish(t):
        for unit, _, _ in halves[t]:
            unit.finish()

    lane = lax.broadcasted_iota(jnp.int32, (8, 128), 1) // 32

    def right_copy(k, zh):
        return pltpu.make_async_remote_copy(
            src_ref=rsend.at[k],
            dst_ref=rrecv.at[p.c],
            send_sem=r_send_sems.at[k * 2 + zh],
            recv_sem=r_recv_sems.at[p.c],
            device_id=(zh * 2 + p.core, p.r * 8 + k),
            device_id_type=MESH,
        )

    def is_remote(k, zh):
        return jnp.logical_or(p.c != p.r * 8 + k, p.zh != zh)

    def send_right(t):
        for k in range(4 * t, 4 * t + 4):
            rows = []
            for half in range(2):
                parts = []
                for q in range(4):
                    j = k * 32 + half * 16 + q * 4
                    v = [rscr[pl.ds(j + u, 8, stride=256), :] for u in range(4)]
                    parts.append(
                        jnp.where(lane == 0, v[0], jnp.where(lane == 1, v[1], jnp.where(lane == 2, v[2], v[3])))
                    )
                parts.append(mask[:, t * 128 : t * 128 + 128])
                rows.append(jnp.concatenate(parts, 1))
            rsend[k] = jnp.concatenate(rows, 0).astype(BF16)

        @pl.loop(0, 8)
        def _(n):
            k, zh = 4 * t + n // 2, lax.rem(n, 2)

            @pl.when(is_remote(k, zh))
            def _():
                right_copy(k, zh).start()

            @pl.when(jnp.logical_not(is_remote(k, zh)))
            def _():
                pltpu.make_async_copy(rsend.at[k], rrecv.at[p.c], r_recv_sems.at[p.c]).start()

    right_pass = pltpu.make_async_remote_copy(
        src_ref=rrecv,
        dst_ref=rrecv,
        send_sem=pass_sems.at[0],
        recv_sem=pass_sems.at[1],
        device_id=core_peer,
        device_id_type=MESH,
    )

    transition_block(0, 0)
    transition_block(0, 1)
    fill_left(0)
    maskall[p.x, p.y, p.zl] = jnp.concatenate([mask, mask], 0).astype(BF16)
    pl.semaphore_wait(barrier, len(greeted) + 16 - (home == p.r).astype(jnp.int32))
    first(0)
    send_right(0)
    transition_block(1, 0)
    transition_block(1, 1)
    fill_left(1)
    second(0)
    first(1)
    send_right(1)
    ow_t = jnp.transpose(ow_ref[...].astype(F32)).astype(BF16)
    second_forward(0)
    second(1)

    @pl.when(receives)
    def _():
        @pl.loop(0, 32)
        def _(c):
            pltpu.make_async_copy(rrecv.at[c], rrecv.at[c], r_recv_sems.at[c]).wait()

        right_pass.start()

    @pl.when(jnp.logical_not(receives))
    def _():
        right_pass.wait_recv()

    place_in_tile = pl.multiple_of(lax.rem(p.c, 4) * 32, 32)
    for half in range(2):
        rows = rrecv[:, :, :].astype(F32)[:, half * 8 : half * 8 + 8, :].reshape(256, 640)
        rt[half * 512 : half * 512 + 512, :] = jnp.transpose(rows[:, :512]).astype(BF16)
        if half == 0:
            col_scr[...] = jnp.transpose(rows[:, 512:])
    mask_j = col_scr[pl.ds(place_in_tile, 32), :].astype(BF16)
    res = res_ref[...].astype(F32)
    rowid = lax.broadcasted_iota(jnp.int32, (8, 128), 0)
    pick = lambda n: jnp.sum(jnp.where(rowid == n, res, 0.0), 0, keepdims=True)
    res_i = jnp.concatenate([pick(p.r * 2), pick(p.r * 2 + 1)], 1)
    res_j = jnp.transpose(jnp.broadcast_to(pick(p.c // 4), (128, 128)))
    col_scr[:, 0:128] = res_j
    res_j = col_scr[pl.ds(place_in_tile, 32), 0:128]

    for t in range(2):
        finish(t)
        if t == 0:
            mask_i = maskall[...].astype(F32)[:, :, :, :8, :].reshape(256, 256).astype(BF16)
            pair_count = jnp.dot(mask_j, mask_i, preferred_element_type=F32) + COUNT_OFFSET
            factor = jnp.concatenate([res_j, res_j], 1) * res_i / pair_count
            counts[0] = factor[:, :128]
            counts[1] = factor[:, 128:]

        @pl.loop(0, 16)
        def _(n):
            x, y = n // 4, lax.rem(n, 4)
            two = raw[t, x, y].astype(F32)
            rows = pl.ds(pl.multiple_of(n * 16, 16), 16)
            for part in range(2):
                both = two[:, part * 8 : part * 8 + 8, :].reshape(16, 2048)
                left[rows, part * 2048 : part * 2048 + 2048] = both.astype(BF16)

        @pl.loop(0, 4)
        def _(n):
            for u in range(4):
                pair = n * 4 + u
                lanes = pl.ds(pl.multiple_of(pair * 256, 256), 256)
                o = jnp.dot(rt[...], left[:, lanes], preferred_element_type=F32).astype(BF16)
                for v in range(2):
                    obuf[:, pair * 2 + v] = o[:, v * 128 : v * 128 + 128].reshape(32, 32, 128)

        if t == 0:
            second_forward(1)

        @pl.loop(0, 4)
        def _(n):
            for u in range(4):
                j = n * 8 + u * 2
                two = jnp.concatenate([obuf[j + v].reshape(1024, 128) for v in range(2)], 1)
                o = jnp.dot(ow_t, two, preferred_element_type=F32)
                for v in range(2):
                    scale = counts[t, pl.ds(j + v, 1), :]
                    upd[pl.ds(t * 4096 + j + v, 128, stride=32), :] = jnp.transpose(o[:, v * 128 : v * 128 + 128] * scale)

        @pl.loop(0, 4)
        def _(n):
            rows = pl.ds(pl.multiple_of(t * 4096 + n * 1024, 1024), 1024)
            out_ref[rows, :] = (pair_ref[rows, :].astype(F32) + upd[rows, :]).astype(BF16)

    sender.wait_sent()

    @pl.when(receives)
    def _():
        right_pass.wait_send()

    @pl.loop(0, 16)
    def _(n):
        k, zh = n // 2, lax.rem(n, 2)

        @pl.when(is_remote(k, zh))
        def _():
            right_copy(k, zh).wait_send()


def vmem(n):
    return [pl.BlockSpec(memory_space=pltpu.VMEM)] * n


def attend(x, pair, mask, w, bw):
    copies = 8 + 3 + 12 + 8 * 7
    return pl.pallas_call(
        attention_kernel,
        out_shape=jax.ShapeDtypeStruct((8, 256, 256), BF16),
        in_specs=vmem(5),
        out_specs=pl.BlockSpec(memory_space=pltpu.VMEM),
        scratch_shapes=[
            pltpu.VMEM((8192, 128), F32),
            pltpu.VMEM((2, 256, 128), F32),
            pltpu.VMEM((8, 4, 4, 64, 256), F32),
            pltpu.VMEM((8, 4, 256, 256), BF16),
            pltpu.VMEM((4, 8, 256), F32),
            pltpu.VMEM((8, 1024, 128), F32),
            pltpu.VMEM((8, 2, 1024, 128), BF16),
            pltpu.VMEM((8, 8, 48, 1024), BF16),
            pltpu.VMEM((8, 256, 256), BF16),
            pltpu.VMEM((8, 256, 256), F32),
            pltpu.VMEM((8, 256, 256), F32),
        ]
        + [pltpu.VMEM((1024, 256), F32)] * 4
        + [pltpu.SemaphoreType.DMA((copies,)), pltpu.SemaphoreType.DMA((copies,))],
        compiler_params=pltpu.CompilerParams(collective_id=0, has_side_effects=True, vmem_limit_bytes=VMEM_BYTES),
    )(x, pair, mask, w, bw)


def transition(x, gated, pair, mask, res, wo, w1, w2, wlr, ow):
    copies = 5 * 11
    return pl.pallas_call(
        transition_kernel,
        out_shape=(
            jax.ShapeDtypeStruct((8, 256, 256), BF16),
            jax.ShapeDtypeStruct((8192, 128), BF16),
        ),
        in_specs=vmem(10),
        out_specs=tuple(vmem(2)),
        scratch_shapes=[
            pltpu.VMEM((2, 256, 128), F32),
            pltpu.VMEM((2048, 128), F32),
            pltpu.VMEM((2, 4, 4, 2, 16, 2048), BF16),
            pltpu.VMEM((256, 4096), BF16),
            pltpu.VMEM((4, 4, 2, 16, 256), BF16),
            pltpu.VMEM((8, 16, 640), BF16),
            pltpu.VMEM((32, 16, 640), BF16),
            pltpu.VMEM((1024, 256), BF16),
            pltpu.VMEM((32, 32, 32, 128), BF16),
            pltpu.VMEM((8192, 128), F32),
            pltpu.VMEM((2, 32, 128), F32),
            pltpu.VMEM((128, 256), F32),
            pltpu.SemaphoreType.DMA((copies,)),
            pltpu.SemaphoreType.DMA((copies,)),
            pltpu.SemaphoreType.DMA((16,)),
            pltpu.SemaphoreType.DMA((32,)),
            pltpu.SemaphoreType.DMA((2,)),
        ],
        compiler_params=pltpu.CompilerParams(collective_id=1, has_side_effects=True, vmem_limit_bytes=VMEM_BYTES),
    )(x, gated, pair, mask, res, wo, w1, w2, wlr, ow)


def per_device(x, pairwise, mask, residue_mask, w, wo, bw, w1, w2, wlr, ow):
    pair = pairwise.reshape(8192, 128)
    gated = attend(x, pair, mask, w, bw.T)
    alignment, new_pair = transition(x, gated, pair, mask, residue_mask.reshape(8, 128), wo, w1, w2, wlr.T, ow)
    return alignment, new_pair.reshape(256, 32, 128)


def solution(mesh):
    return jax.shard_map(
        per_device,
        mesh=mesh,
        in_specs=(P("col", "row", None), P("row", "col", None), P("col", "row")) + (P(),) * 8,
        out_specs=(P("col", "row", None), P("row", "col", None)),
        check_vma=False,
    )
```

```python
import functools

import jax
import jax.numpy as jnp
from jax import lax
from jax.experimental import pallas as pl
from jax.experimental.pallas import tpu as pltpu
from jax.sharding import PartitionSpec as P

MESH = pl.DeviceIdType.MESH
F32 = jnp.float32
BF16 = jnp.bfloat16
EPS = 1e-05
LOG2E = 1.4426950408889634
MASKED = 1000000000.0
COUNT_OFFSET = 0.001
HEADS = 8
NT = (((1,), (1,)), ((), ()))
VMEM_BYTES = 60 * 2**20


def layer_norm(v):
    d = v - jnp.mean(v, -1, keepdims=True)
    return d * lax.rsqrt(jnp.mean(d * d, -1, keepdims=True) + EPS)


class Place:
    def __init__(self):
        self.r = lax.axis_index("row")
        self.c = lax.axis_index("col")
        self.zh, self.core = self.r // 2, lax.rem(self.r, 2)
        self.x, self.y = self.c // 8, lax.rem(self.c // 2, 4)
        self.zl = lax.rem(self.c, 2)
        self.xp, self.xm = lax.rem(self.x + 1, 4), lax.rem(self.x + 3, 4)
        self.yp, self.ym = lax.rem(self.y + 1, 4), lax.rem(self.y + 3, 4)
        self.xo, self.yo = lax.rem(self.x + 2, 4), lax.rem(self.y + 2, 4)

    def along(self, on_x):
        if on_x:
            return [self.at(x=x) for x in (self.xp, self.xm, self.xo)]
        return [self.at(y=y) for y in (self.yp, self.ym, self.yo)]

    def along_with_pair(self, on_x):
        other = 1 - self.zl
        if on_x:
            return self.along(True) + [self.at(x=x, zl=other) for x in (self.x, self.xp, self.xm, self.xo)]
        return self.along(False) + [self.at(y=y, zl=other) for y in (self.y, self.yp, self.ym, self.yo)]

    def at(self, zh=None, core=None, x=None, y=None, zl=None):
        zh = self.zh if zh is None else zh
        core = self.core if core is None else core
        x = self.x if x is None else x
        y = self.y if y is None else y
        zl = self.zl if zl is None else zl
        return (zh * 2 + core, (x * 4 + y) * 2 + zl)


class Sender:
    def __init__(self, send_sems, recv_sems):
        self.send_sems, self.recv_sems, self.copies = send_sems, recv_sems, []

    def start(self, src, dst, device):
        n = len(self.copies)
        copy = pltpu.make_async_remote_copy(
            src_ref=src,
            dst_ref=dst,
            send_sem=self.send_sems.at[n],
            recv_sem=self.recv_sems.at[n],
            device_id=device,
            device_id_type=MESH,
        )
        copy.start()
        self.copies.append(copy)
        return copy

    def wait_sent(self):
        for copy in self.copies:
            copy.wait_send()


class PlaneGather:
    def __init__(self, place, sender, view, x_first):
        self.p, self.s, self.view, self.x_first = place, sender, view, x_first
        self.pending = ()

    def _ring(self, plus, minus):
        p = self.p
        up = p.at(y=p.yp) if self.x_first else p.at(x=p.xp)
        down = p.at(y=p.ym) if self.x_first else p.at(x=p.xm)
        self.pending = (self.s.start(plus, plus, up), self.s.start(minus, minus, down))

    def _wait(self):
        for copy in self.pending:
            copy.wait_recv()

    def first(self, own, devices):
        self.pending = tuple(self.s.start(own, own, device) for device in devices)

    def second(self):
        p = self.p
        self._wait()
        every = slice(0, 4)
        line = self.view(every, p.y) if self.x_first else self.view(p.x, every)
        self._ring(line, line)

    def second_forward(self):
        p = self.p
        self._wait()
        low, high = slice(0, 2), slice(2, 4)
        if self.x_first:
            self._ring(self.view(low, p.ym), self.view(high, p.yp))
        else:
            self._ring(self.view(p.xm, low), self.view(p.xp, high))

    def finish(self):
        self._wait()


def window(index):
    return pl.ds(index.start, index.stop - index.start) if isinstance(index, slice) else index


def greet(devices):
    barrier = pltpu.get_barrier_semaphore()
    for device in devices:
        pl.semaphore_signal(barrier, inc=1, device_id=device, device_id_type=MESH)
    return barrier


def fold_max(v):
    parts = [v[8 * i : 8 * i + 8] for i in range(v.shape[0] // 8)]
    while len(parts) > 1:
        parts = [
            jnp.maximum(parts[i], parts[i + 1]) if i + 1 < len(parts) else parts[i]
            for i in range(0, len(parts), 2)
        ]
    return parts[0]


def attention_kernel(
    x_ref, pair_ref, mask_ref, w_ref, bw_ref,
    out_ref,
    pair32, stage, bias, xg, maskg, maskb, kt, vt, qt, gate, att,
    s0, s1, s2, s3, send_sems, recv_sems,
):
    p = Place()
    peers = p.along(True) + p.along(False) + [p.at(zl=1 - p.zl), p.at(core=1 - p.core), p.at(zh=1 - p.zh)]
    barrier = greet(peers)
    sender = Sender(send_sems, recv_sems)

    pair32[...] = pair_ref[...].astype(F32)
    bw = bw_ref[...] * LOG2E
    bw_high = bw.astype(BF16)
    bw_low = (bw - bw_high.astype(F32)).astype(BF16)
    bw_rows = jnp.concatenate([bw_high, bw_low], 0)
    bw_both = jnp.concatenate([bw_rows, bw_rows], 1)

    @pl.loop(0, 8)
    def _(jb):
        for u in range(4):
            j = jb * 4 + u
            n = layer_norm(pair32[pl.ds(j, 256, stride=32), :])
            high = n.astype(BF16)
            low = (n - high.astype(F32)).astype(BF16)
            both = jnp.concatenate([high, low], 1)
            r = lax.dot_general(bw_both, both, NT, preferred_element_type=F32)
            r = r[:8] + r[8:]
            for t in range(2):
                stage[t, pl.ds(j, 8, stride=32), :] = r[:, t * 128 : t * 128 + 128]

    for h in range(HEADS):
        rows = slice(h * 32, h * 32 + 32)
        bias[h, p.x, p.y, pl.ds(p.zl * 32, 32), :] = jnp.concatenate([stage[0, rows, :], stage[1, rows, :]], 1)
    pl.semaphore_wait(barrier, len(peers))

    z_copies = {}

    def to_pair(k):
        for h in (2 * k, 2 * k + 1):
            own = bias.at[h, p.x, p.y, pl.ds(p.zl * 32, 32)]
            z_copies[h] = sender.start(own, own, p.at(zl=1 - p.zl))

    to_pair(0)

    def head_view(h):
        return lambda x, y: bias.at[h, window(x), window(y)]

    gathers = [PlaneGather(p, sender, head_view(h), h % 2 == 0) for h in range(HEADS)]

    def first(k):
        for h in (2 * k, 2 * k + 1):
            z_copies[h].wait_recv()
            gathers[h].first(bias.at[h, p.x, p.y], p.along(h % 2 == 0))

    def second(k):
        for h in (2 * k, 2 * k + 1):
            gathers[h].second()

    def second_forward(k):
        for h in (2 * k, 2 * k + 1):
            gathers[h].second_forward()

    def finish(k):
        for h in (2 * k, 2 * k + 1):
            gathers[h].finish()

    def normalise(s):
        xg[s, p.r] = layer_norm(x_ref[s].astype(F32)).astype(BF16)

    core_peer, z_peer = p.at(core=1 - p.core), p.at(zh=1 - p.zh)
    far = (1 - p.zh) * 2 + p.core
    near_copies, far_copies, pass_copies = [], [], []

    def share(g):
        own = xg.at[pl.ds(2 * g, 2), p.r]
        far_copies.append(sender.start(own, own, z_peer))
        near_copies.append(sender.start(own, own, core_peer))

    wq = w_ref[:, 0:256]
    wk = w_ref[:, 256:512]
    wv = w_ref[:, 512:768]
    wg = w_ref[:, 768:1024]
    wq_t = jnp.transpose(wq.astype(F32)).astype(BF16)
    wv_t = jnp.transpose(wv.astype(F32)).astype(BF16)

    def project(s):
        own = xg[s, p.r]
        q = lax.dot_general(wq_t, own, NT, preferred_element_type=F32)
        qt[s] = (q * (LOG2E * 32**-0.5)).astype(BF16)
        gate[s] = jax.nn.sigmoid(jnp.dot(own, wg, preferred_element_type=F32))

    for s in range(4):
        normalise(s)
    first(0)
    to_pair(1)
    for s in range(4, 8):
        normalise(s)
    share(0)
    maskg[p.r] = (mask_ref[...].astype(F32) - 1.0) * (MASKED * LOG2E)
    mask_copies = [
        sender.start(maskg.at[p.r], maskg.at[p.r], core_peer),
        sender.start(maskg.at[p.r], maskg.at[p.r], z_peer),
    ]
    for s in range(4):
        project(s)
    second(0)
    first(1)
    to_pair(2)
    to_pair(3)
    share(1)
    for s in range(4, 8):
        project(s)
    first(2)
    second(1)
    for copy in mask_copies:
        copy.wait_recv()
    mask_copies.append(sender.start(maskg.at[far], maskg.at[far], core_peer))
    mask_copies[2].wait_recv()
    for r in range(4):
        columns = jnp.transpose(maskg[r])
        for s in range(8):
            maskb[s, r * 256 : r * 256 + 256, :] = jnp.broadcast_to(columns[:, s : s + 1], (256, 128))

    vt[:, :, 32:48, :] = jnp.ones((8, 8, 16, 1024), BF16)
    def pass_on(g):
        far_copies[g].wait_recv()
        piece = xg.at[pl.ds(2 * g, 2), far]
        pass_copies.append(sender.start(piece, piece, core_peer))

    def project_all(g):
        near_copies[g].wait_recv()
        pass_copies[g].wait_recv()

        @pl.loop(2 * g, 2 * g + 2)
        def _(s):
            for r in range(4):
                rows = xg[s, r]
                k = jnp.dot(rows, wk, preferred_element_type=F32).astype(BF16)
                kt[s, 0, r * 256 : r * 256 + 256, :] = k[:, :128]
                kt[s, 1, r * 256 : r * 256 + 256, :] = k[:, 128:]
                v = lax.dot_general(wv_t, rows, NT, preferred_element_type=F32).astype(BF16)
                vt[s, :, 0:32, r * 256 : r * 256 + 256] = v.reshape(8, 32, 256)

    head_of = lax.broadcasted_iota(jnp.int32, (128, 256), 0) // 32

    def step(new, new_scores, now, now_scores, now_max):
        new_max, total = [None, None], [None, None]
        if new is not None:
            h, first = new
            tile = h // 4
            q = [
                jnp.where(
                    head_of == h % 4, qt[first + u, tile * 128 : tile * 128 + 128, :].astype(F32), 0.0
                ).astype(BF16)
                for u in range(2)
            ]
        for jc in range(4):
            rows = slice(jc * 256, jc * 256 + 256)
            if new is not None:
                b = bias[h, jc].reshape(256, 256)
                for u in range(2):
                    m = maskb[first + u, rows, :]
                    sc = jnp.dot(kt[first + u, tile, rows, :], q[u], preferred_element_type=F32)
                    sc = sc + b + jnp.concatenate([m, m], 1)
                    new_scores[u][rows, :] = sc
                    f = fold_max(sc)
                    new_max[u] = f if new_max[u] is None else jnp.maximum(new_max[u], f)
            if now is not None:
                hn, start = now
                for u in range(2):
                    e = jnp.exp2(now_scores[u][rows, :] - now_max[u]).astype(BF16)
                    a = jnp.dot(vt[start + u, hn, :, rows], e, preferred_element_type=F32)
                    total[u] = a if total[u] is None else total[u] + a
        if now is not None:
            for u in range(2):
                att[start + u, hn * 32 : hn * 32 + 32, :] = total[u][:32] / total[u][32:33]
        if new is not None:
            return tuple(jnp.max(m, axis=0, keepdims=True) for m in new_max)

    sets = ((s0, s1), (s2, s3))
    last = [None, None, 0]

    def attend_to(*items):
        for new in items:
            now, top, n = last
            number = n + 1
            scores = sets[number % 2]
            last[:] = new, step(new, scores, now, sets[n % 2], top), number

    second_forward(0)
    second(2)
    first(3)
    pass_on(0)
    share(2)
    pass_on(1)
    project_all(0)
    share(3)
    pass_on(2)
    project_all(1)
    second_forward(1)
    second(3)
    finish(0)
    pass_on(3)
    attend_to((0, 0), (0, 2), (1, 0), (1, 2))
    project_all(2)
    attend_to((0, 4), (1, 4))
    project_all(3)
    second_forward(2)
    attend_to((0, 6), (1, 6))
    finish(1)
    attend_to((2, 0), (2, 2), (2, 4), (2, 6))
    second_forward(3)
    attend_to((3, 0), (3, 2), (3, 4), (3, 6))
    for k in (2, 3):
        finish(k)
        attend_to(*((h, 2 * g) for h in (2 * k, 2 * k + 1) for g in range(4)))
    step(None, None, last[0], sets[last[2] % 2], last[1])

    for s in range(8):
        out_ref[s] = (jnp.transpose(att[s]) * gate[s]).astype(BF16)
    sender.wait_sent()


def transition_kernel(
    x_ref, gated_ref, pair_ref, mask_ref, res_ref, wo_ref, w1_ref, w2_ref, wlr_ref, ow_ref,
    align_ref, out_ref,
    lscr, rscr, raw, left, maskall, rsend, rrecv, rt, obuf, upd, counts, col_scr,
    send_sems, recv_sems, r_send_sems, r_recv_sems, pass_sems,
):
    p = Place()
    home = p.c // 8
    core_peer = p.at(core=1 - p.core)
    receives = lax.rem(home, 2) == p.core
    greeted = p.along_with_pair(True) + p.along_with_pair(False) + [core_peer]
    barrier = greet(greeted)

    @pl.loop(0, 32)
    def _(c):
        @pl.when(jnp.logical_and(receives, jnp.logical_or(home != p.r, c != p.c)))
        def _():
            pl.semaphore_signal(barrier, inc=1, device_id=(home, c), device_id_type=MESH)

    sender = Sender(send_sems, recv_sems)
    mask = mask_ref[...].astype(F32)

    wl_t = wlr_ref[0:32, :]
    wr = wlr_ref[32:64, :]
    wr4 = jnp.concatenate([wr, wr, wr, wr], 0)
    mask_cols = jnp.transpose(mask)

    def transition_block(t, q):
        half = slice(t * 128, t * 128 + 128)
        four = slice(4 * q, 4 * q + 4)
        rows = x_ref[four, half, :].reshape(512, 256).astype(F32)
        gated = gated_ref[four, half, :].reshape(512, 256)
        after = rows + jnp.dot(gated, wo_ref[...], preferred_element_type=F32)
        hidden = jnp.dot(layer_norm(after).astype(BF16), w1_ref[...], preferred_element_type=F32)
        hidden = jnp.maximum(hidden, 0.0).astype(BF16)
        after = after + jnp.dot(hidden, w2_ref[...], preferred_element_type=F32)
        align_ref[four, half, :] = after.astype(BF16).reshape(4, 128, 256)
        n = layer_norm(after).astype(BF16)
        l = lax.dot_general(wl_t, n, NT, preferred_element_type=F32)
        rr = lax.dot_general(n, wr4, NT, preferred_element_type=F32)
        for u in range(4):
            s = 4 * q + u
            cols = slice(u * 128, u * 128 + 128)
            lscr[t, s * 32 : s * 32 + 32, :] = l[:, cols] * mask[s : s + 1, half]
            start = s * 256 + t * 128
            rscr[start : start + 128, :] = rr[cols] * mask_cols[half, s : s + 1]

    def own_left(t, a):
        return lscr[t, pl.ds(a, 8, stride=32), :]

    def fill_left(t):
        for a in range(16):
            both = jnp.concatenate([own_left(t, a), own_left(t, a + 16)], 0)
            raw[t, p.x, p.y, p.zl, :, a * 128 : a * 128 + 128] = both.astype(BF16)

    def left_part(t, part):
        lanes = pl.ds(part * 1024, 1024)
        view = lambda x, y: raw.at[t, window(x), window(y), pl.ds(0, 2), pl.ds(0, 16), lanes]
        own = raw.at[t, p.x, p.y, p.zl, pl.ds(0, 16), lanes]
        return PlaneGather(p, sender, view, part == 0), own, p.along_with_pair(part == 0)

    def mask_view(x, y):
        return maskall.at[window(x), window(y), pl.ds(0, 2), pl.ds(0, 16)]

    mask_unit = (
        PlaneGather(p, sender, mask_view, False),
        maskall.at[p.x, p.y, p.zl, pl.ds(0, 16)],
        p.along_with_pair(False),
    )
    halves = [[left_part(0, 0), left_part(0, 1), mask_unit], [left_part(1, 0), left_part(1, 1)]]

    def first(t):
        for unit, own, devices in halves[t]:
            unit.first(own, devices)

    def second(t):
        for unit, _, _ in halves[t]:
            unit.second()

    def second_forward(t):
        for unit, _, _ in halves[t]:
            unit.second_forward()

    def finish(t):
        for unit, _, _ in halves[t]:
            unit.finish()

    lane = lax.broadcasted_iota(jnp.int32, (8, 128), 1) // 32

    def right_copy(k, zh):
        return pltpu.make_async_remote_copy(
            src_ref=rsend.at[k],
            dst_ref=rrecv.at[p.c],
            send_sem=r_send_sems.at[k * 2 + zh],
            recv_sem=r_recv_sems.at[p.c],
            device_id=(zh * 2 + p.core, p.r * 8 + k),
            device_id_type=MESH,
        )

    def is_remote(k, zh):
        return jnp.logical_or(p.c != p.r * 8 + k, p.zh != zh)

    def send_right(t):
        for k in range(4 * t, 4 * t + 4):
            rows = []
            for half in range(2):
                parts = []
                for q in range(4):
                    j = k * 32 + half * 16 + q * 4
                    v = [rscr[pl.ds(j + u, 8, stride=256), :] for u in range(4)]
                    parts.append(
                        jnp.where(lane == 0, v[0], jnp.where(lane == 1, v[1], jnp.where(lane == 2, v[2], v[3])))
                    )
                parts.append(mask[:, t * 128 : t * 128 + 128])
                rows.append(jnp.concatenate(parts, 1))
            rsend[k] = jnp.concatenate(rows, 0).astype(BF16)

        @pl.loop(0, 8)
        def _(n):
            k, zh = 4 * t + n // 2, lax.rem(n, 2)

            @pl.when(is_remote(k, zh))
            def _():
                right_copy(k, zh).start()

            @pl.when(jnp.logical_not(is_remote(k, zh)))
            def _():
                pltpu.make_async_copy(rsend.at[k], rrecv.at[p.c], r_recv_sems.at[p.c]).start()

    right_pass = pltpu.make_async_remote_copy(
        src_ref=rrecv,
        dst_ref=rrecv,
        send_sem=pass_sems.at[0],
        recv_sem=pass_sems.at[1],
        device_id=core_peer,
        device_id_type=MESH,
    )

    transition_block(0, 0)
    transition_block(0, 1)
    fill_left(0)
    maskall[p.x, p.y, p.zl] = jnp.concatenate([mask, mask], 0).astype(BF16)
    pl.semaphore_wait(barrier, len(greeted) + 16 - (home == p.r).astype(jnp.int32))
    first(0)
    send_right(0)
    transition_block(1, 0)
    transition_block(1, 1)
    fill_left(1)
    second(0)
    first(1)
    send_right(1)
    ow_t = jnp.transpose(ow_ref[...].astype(F32)).astype(BF16)
    second_forward(0)
    second(1)

    @pl.when(receives)
    def _():
        @pl.loop(0, 32)
        def _(c):
            pltpu.make_async_copy(rrecv.at[c], rrecv.at[c], r_recv_sems.at[c]).wait()

        right_pass.start()

    @pl.when(jnp.logical_not(receives))
    def _():
        right_pass.wait_recv()

    place_in_tile = pl.multiple_of(lax.rem(p.c, 4) * 32, 32)
    for half in range(2):
        rows = rrecv[:, :, :].astype(F32)[:, half * 8 : half * 8 + 8, :].reshape(256, 640)
        rt[half * 512 : half * 512 + 512, :] = jnp.transpose(rows[:, :512]).astype(BF16)
        if half == 0:
            col_scr[...] = jnp.transpose(rows[:, 512:])
    mask_j = col_scr[pl.ds(place_in_tile, 32), :].astype(BF16)
    res = res_ref[...].astype(F32)
    rowid = lax.broadcasted_iota(jnp.int32, (8, 128), 0)
    pick = lambda n: jnp.sum(jnp.where(rowid == n, res, 0.0), 0, keepdims=True)
    res_i = jnp.concatenate([pick(p.r * 2), pick(p.r * 2 + 1)], 1)
    res_j = jnp.transpose(jnp.broadcast_to(pick(p.c // 4), (128, 128)))
    col_scr[:, 0:128] = res_j
    res_j = col_scr[pl.ds(place_in_tile, 32), 0:128]

    for t in range(2):
        finish(t)
        if t == 0:
            mask_i = maskall[...].astype(F32)[:, :, :, :8, :].reshape(256, 256).astype(BF16)
            pair_count = jnp.dot(mask_j, mask_i, preferred_element_type=F32) + COUNT_OFFSET
            factor = jnp.concatenate([res_j, res_j], 1) * res_i / pair_count
            counts[0] = factor[:, :128]
            counts[1] = factor[:, 128:]

        @pl.loop(0, 16)
        def _(n):
            x, y = n // 4, lax.rem(n, 4)
            two = raw[t, x, y].astype(F32)
            rows = pl.ds(pl.multiple_of(n * 16, 16), 16)
            for part in range(2):
                both = two[:, part * 8 : part * 8 + 8, :].reshape(16, 2048)
                left[rows, part * 2048 : part * 2048 + 2048] = both.astype(BF16)

        @pl.loop(0, 4)
        def _(n):
            for u in range(4):
                pair = n * 4 + u
                lanes = pl.ds(pl.multiple_of(pair * 256, 256), 256)
                o = jnp.dot(rt[...], left[:, lanes], preferred_element_type=F32).astype(BF16)
                for v in range(2):
                    obuf[:, pair * 2 + v] = o[:, v * 128 : v * 128 + 128].reshape(32, 32, 128)

        if t == 0:
            second_forward(1)

        @pl.loop(0, 4)
        def _(n):
            for u in range(4):
                j = n * 8 + u * 2
                two = jnp.concatenate([obuf[j + v].reshape(1024, 128) for v in range(2)], 1)
                o = jnp.dot(ow_t, two, preferred_element_type=F32)
                for v in range(2):
                    scale = counts[t, pl.ds(j + v, 1), :]
                    upd[pl.ds(t * 4096 + j + v, 128, stride=32), :] = jnp.transpose(o[:, v * 128 : v * 128 + 128] * scale)

        @pl.loop(0, 4)
        def _(n):
            rows = pl.ds(pl.multiple_of(t * 4096 + n * 1024, 1024), 1024)
            out_ref[rows, :] = (pair_ref[rows, :].astype(F32) + upd[rows, :]).astype(BF16)

    sender.wait_sent()

    @pl.when(receives)
    def _():
        right_pass.wait_send()

    @pl.loop(0, 16)
    def _(n):
        k, zh = n // 2, lax.rem(n, 2)

        @pl.when(is_remote(k, zh))
        def _():
            right_copy(k, zh).wait_send()


def vmem(n):
    return [pl.BlockSpec(memory_space=pltpu.VMEM)] * n


def attend(x, pair, mask, w, bw):
    copies = 8 + 3 + 12 + 8 * 7
    return pl.pallas_call(
        attention_kernel,
        out_shape=jax.ShapeDtypeStruct((8, 256, 256), BF16),
        in_specs=vmem(5),
        out_specs=pl.BlockSpec(memory_space=pltpu.VMEM),
        scratch_shapes=[
            pltpu.VMEM((8192, 128), F32),
            pltpu.VMEM((2, 256, 128), F32),
            pltpu.VMEM((8, 4, 4, 64, 256), F32),
            pltpu.VMEM((8, 4, 256, 256), BF16),
            pltpu.VMEM((4, 8, 256), F32),
            pltpu.VMEM((8, 1024, 128), F32),
            pltpu.VMEM((8, 2, 1024, 128), BF16),
            pltpu.VMEM((8, 8, 48, 1024), BF16),
            pltpu.VMEM((8, 256, 256), BF16),
            pltpu.VMEM((8, 256, 256), F32),
            pltpu.VMEM((8, 256, 256), F32),
        ]
        + [pltpu.VMEM((1024, 256), F32)] * 4
        + [pltpu.SemaphoreType.DMA((copies,)), pltpu.SemaphoreType.DMA((copies,))],
        compiler_params=pltpu.CompilerParams(collective_id=0, has_side_effects=True, vmem_limit_bytes=VMEM_BYTES),
    )(x, pair, mask, w, bw)


def transition(x, gated, pair, mask, res, wo, w1, w2, wlr, ow):
    copies = 5 * 11
    return pl.pallas_call(
        transition_kernel,
        out_shape=(
            jax.ShapeDtypeStruct((8, 256, 256), BF16),
            jax.ShapeDtypeStruct((8192, 128), BF16),
        ),
        in_specs=vmem(10),
        out_specs=tuple(vmem(2)),
        scratch_shapes=[
            pltpu.VMEM((2, 256, 128), F32),
            pltpu.VMEM((2048, 128), F32),
            pltpu.VMEM((2, 4, 4, 2, 16, 2048), BF16),
            pltpu.VMEM((256, 4096), BF16),
            pltpu.VMEM((4, 4, 2, 16, 256), BF16),
            pltpu.VMEM((8, 16, 640), BF16),
            pltpu.VMEM((32, 16, 640), BF16),
            pltpu.VMEM((1024, 256), BF16),
            pltpu.VMEM((32, 32, 32, 128), BF16),
            pltpu.VMEM((8192, 128), F32),
            pltpu.VMEM((2, 32, 128), F32),
            pltpu.VMEM((128, 256), F32),
            pltpu.SemaphoreType.DMA((copies,)),
            pltpu.SemaphoreType.DMA((copies,)),
            pltpu.SemaphoreType.DMA((16,)),
            pltpu.SemaphoreType.DMA((32,)),
            pltpu.SemaphoreType.DMA((2,)),
        ],
        compiler_params=pltpu.CompilerParams(collective_id=1, has_side_effects=True, vmem_limit_bytes=VMEM_BYTES),
    )(x, gated, pair, mask, res, wo, w1, w2, wlr, ow)


def per_device(x, pairwise, mask, residue_mask, w, wo, bw, w1, w2, wlr, ow):
    pair = pairwise.reshape(8192, 128)
    gated = attend(x, pair, mask, w, bw.T)
    alignment, new_pair = transition(x, gated, pair, mask, residue_mask.reshape(8, 128), wo, w1, w2, wlr.T, ow)
    return alignment, new_pair.reshape(256, 32, 128)


def solution(mesh):
    return jax.shard_map(
        per_device,
        mesh=mesh,
        in_specs=(P("col", "row", None), P("row", "col", None), P("col", "row")) + (P(),) * 8,
        out_specs=(P("col", "row", None), P("row", "col", None)),
        check_vma=False,
    )
```

```python
import functools

import jax
import jax.numpy as jnp
from jax import lax
from jax.experimental import pallas as pl
from jax.experimental.pallas import tpu as pltpu
from jax.sharding import PartitionSpec as P

MESH = pl.DeviceIdType.MESH
F32 = jnp.float32
BF16 = jnp.bfloat16
EPS = 1e-05
LOG2E = 1.4426950408889634
MASKED = 1000000000.0
COUNT_OFFSET = 0.001
HEADS = 8
NT = (((1,), (1,)), ((), ()))
VMEM_BYTES = 60 * 2**20


def layer_norm(v):
    d = v - jnp.mean(v, -1, keepdims=True)
    return d * lax.rsqrt(jnp.mean(d * d, -1, keepdims=True) + EPS)


class Place:
    def __init__(self):
        self.r = lax.axis_index("row")
        self.c = lax.axis_index("col")
        self.zh, self.core = self.r // 2, lax.rem(self.r, 2)
        self.x, self.y = self.c // 8, lax.rem(self.c // 2, 4)
        self.zl = lax.rem(self.c, 2)
        self.xp, self.xm = lax.rem(self.x + 1, 4), lax.rem(self.x + 3, 4)
        self.yp, self.ym = lax.rem(self.y + 1, 4), lax.rem(self.y + 3, 4)
        self.xo, self.yo = lax.rem(self.x + 2, 4), lax.rem(self.y + 2, 4)

    def along(self, on_x):
        if on_x:
            return [self.at(x=x) for x in (self.xp, self.xm, self.xo)]
        return [self.at(y=y) for y in (self.yp, self.ym, self.yo)]

    def along_with_pair(self, on_x):
        other = 1 - self.zl
        if on_x:
            return self.along(True) + [self.at(x=x, zl=other) for x in (self.x, self.xp, self.xm, self.xo)]
        return self.along(False) + [self.at(y=y, zl=other) for y in (self.y, self.yp, self.ym, self.yo)]

    def at(self, zh=None, core=None, x=None, y=None, zl=None):
        zh = self.zh if zh is None else zh
        core = self.core if core is None else core
        x = self.x if x is None else x
        y = self.y if y is None else y
        zl = self.zl if zl is None else zl
        return (zh * 2 + core, (x * 4 + y) * 2 + zl)


class Sender:
    def __init__(self, send_sems, recv_sems):
        self.send_sems, self.recv_sems, self.copies = send_sems, recv_sems, []

    def start(self, src, dst, device):
        n = len(self.copies)
        copy = pltpu.make_async_remote_copy(
            src_ref=src,
            dst_ref=dst,
            send_sem=self.send_sems.at[n],
            recv_sem=self.recv_sems.at[n],
            device_id=device,
            device_id_type=MESH,
        )
        copy.start()
        self.copies.append(copy)
        return copy

    def wait_sent(self):
        for copy in self.copies:
            copy.wait_send()


class PlaneGather:
    def __init__(self, place, sender, view, x_first):
        self.p, self.s, self.view, self.x_first = place, sender, view, x_first
        self.pending = ()

    def _ring(self, plus, minus):
        p = self.p
        up = p.at(y=p.yp) if self.x_first else p.at(x=p.xp)
        down = p.at(y=p.ym) if self.x_first else p.at(x=p.xm)
        self.pending = (self.s.start(plus, plus, up), self.s.start(minus, minus, down))

    def _wait(self):
        for copy in self.pending:
            copy.wait_recv()

    def first(self, own, devices):
        self.pending = tuple(self.s.start(own, own, device) for device in devices)

    def second(self):
        p = self.p
        self._wait()
        every = slice(0, 4)
        line = self.view(every, p.y) if self.x_first else self.view(p.x, every)
        self._ring(line, line)

    def second_forward(self):
        p = self.p
        self._wait()
        low, high = slice(0, 2), slice(2, 4)
        if self.x_first:
            self._ring(self.view(low, p.ym), self.view(high, p.yp))
        else:
            self._ring(self.view(p.xm, low), self.view(p.xp, high))

    def finish(self):
        self._wait()


def window(index):
    return pl.ds(index.start, index.stop - index.start) if isinstance(index, slice) else index


def greet(devices):
    barrier = pltpu.get_barrier_semaphore()
    for device in devices:
        pl.semaphore_signal(barrier, inc=1, device_id=device, device_id_type=MESH)
    return barrier


def fold_max(v):
    parts = [v[8 * i : 8 * i + 8] for i in range(v.shape[0] // 8)]
    while len(parts) > 1:
        parts = [
            jnp.maximum(parts[i], parts[i + 1]) if i + 1 < len(parts) else parts[i]
            for i in range(0, len(parts), 2)
        ]
    return parts[0]


def attention_kernel(
    x_ref, pair_ref, mask_ref, w_ref, bw_ref,
    out_ref,
    pair32, stage, bias, xg, maskg, maskb, kt, vt, qt, gate, att,
    s0, s1, s2, s3, send_sems, recv_sems,
):
    p = Place()
    peers = p.along(True) + p.along(False) + [p.at(zl=1 - p.zl), p.at(core=1 - p.core), p.at(zh=1 - p.zh)]
    barrier = greet(peers)
    sender = Sender(send_sems, recv_sems)

    pair32[...] = pair_ref[...].astype(F32)
    bw = bw_ref[...] * LOG2E
    bw_high = bw.astype(BF16)
    bw_low = (bw - bw_high.astype(F32)).astype(BF16)
    bw_rows = jnp.concatenate([bw_high, bw_low], 0)
    bw_both = jnp.concatenate([bw_rows, bw_rows], 1)

    @pl.loop(0, 8)
    def _(jb):
        for u in range(4):
            j = jb * 4 + u
            n = layer_norm(pair32[pl.ds(j, 256, stride=32), :])
            high = n.astype(BF16)
            low = (n - high.astype(F32)).astype(BF16)
            both = jnp.concatenate([high, low], 1)
            r = lax.dot_general(bw_both, both, NT, preferred_element_type=F32)
            r = r[:8] + r[8:]
            for t in range(2):
                stage[t, pl.ds(j, 8, stride=32), :] = r[:, t * 128 : t * 128 + 128]

    for h in range(HEADS):
        rows = slice(h * 32, h * 32 + 32)
        bias[h, p.x, p.y, pl.ds(p.zl * 32, 32), :] = jnp.concatenate([stage[0, rows, :], stage[1, rows, :]], 1)
    pl.semaphore_wait(barrier, len(peers))

    z_copies = {}

    def to_pair(k):
        for h in (2 * k, 2 * k + 1):
            own = bias.at[h, p.x, p.y, pl.ds(p.zl * 32, 32)]
            z_copies[h] = sender.start(own, own, p.at(zl=1 - p.zl))

    to_pair(0)

    def head_view(h):
        return lambda x, y: bias.at[h, window(x), window(y)]

    gathers = [PlaneGather(p, sender, head_view(h), h % 2 == 0) for h in range(HEADS)]

    def first(k):
        for h in (2 * k, 2 * k + 1):
            z_copies[h].wait_recv()
            gathers[h].first(bias.at[h, p.x, p.y], p.along(h % 2 == 0))

    def second(k):
        for h in (2 * k, 2 * k + 1):
            gathers[h].second()

    def second_forward(k):
        for h in (2 * k, 2 * k + 1):
            gathers[h].second_forward()

    def finish(k):
        for h in (2 * k, 2 * k + 1):
            gathers[h].finish()

    def normalise(s):
        xg[s, p.r] = layer_norm(x_ref[s].astype(F32)).astype(BF16)

    core_peer, z_peer = p.at(core=1 - p.core), p.at(zh=1 - p.zh)
    far = (1 - p.zh) * 2 + p.core
    near_copies, far_copies, pass_copies = [], [], []

    def share(g):
        own = xg.at[pl.ds(2 * g, 2), p.r]
        far_copies.append(sender.start(own, own, z_peer))
        near_copies.append(sender.start(own, own, core_peer))

    wq = w_ref[:, 0:256]
    wk = w_ref[:, 256:512]
    wv = w_ref[:, 512:768]
    wg = w_ref[:, 768:1024]
    wq_t = jnp.transpose(wq.astype(F32)).astype(BF16)
    wv_t = jnp.transpose(wv.astype(F32)).astype(BF16)

    def project(s):
        own = xg[s, p.r]
        q = lax.dot_general(wq_t, own, NT, preferred_element_type=F32)
        qt[s] = (q * (LOG2E * 32**-0.5)).astype(BF16)
        gate[s] = jax.nn.sigmoid(jnp.dot(own, wg, preferred_element_type=F32))

    for s in range(4):
        normalise(s)
    first(0)
    to_pair(1)
    for s in range(4, 8):
        normalise(s)
    share(0)
    maskg[p.r] = (mask_ref[...].astype(F32) - 1.0) * (MASKED * LOG2E)
    mask_copies = [
        sender.start(maskg.at[p.r], maskg.at[p.r], core_peer),
        sender.start(maskg.at[p.r], maskg.at[p.r], z_peer),
    ]
    for s in range(4):
        project(s)
    second(0)
    first(1)
    to_pair(2)
    to_pair(3)
    share(1)
    for s in range(4, 8):
        project(s)
    first(2)
    second(1)
    for copy in mask_copies:
        copy.wait_recv()
    mask_copies.append(sender.start(maskg.at[far], maskg.at[far], core_peer))
    mask_copies[2].wait_recv()
    for r in range(4):
        columns = jnp.transpose(maskg[r])
        for s in range(8):
            maskb[s, r * 256 : r * 256 + 256, :] = jnp.broadcast_to(columns[:, s : s + 1], (256, 128))

    vt[:, :, 32:48, :] = jnp.ones((8, 8, 16, 1024), BF16)
    def pass_on(g):
        far_copies[g].wait_recv()
        piece = xg.at[pl.ds(2 * g, 2), far]
        pass_copies.append(sender.start(piece, piece, core_peer))

    def project_all(g):
        near_copies[g].wait_recv()
        pass_copies[g].wait_recv()

        @pl.loop(2 * g, 2 * g + 2)
        def _(s):
            for r in range(4):
                rows = xg[s, r]
                k = jnp.dot(rows, wk, preferred_element_type=F32).astype(BF16)
                kt[s, 0, r * 256 : r * 256 + 256, :] = k[:, :128]
                kt[s, 1, r * 256 : r * 256 + 256, :] = k[:, 128:]
                v = lax.dot_general(wv_t, rows, NT, preferred_element_type=F32).astype(BF16)
                vt[s, :, 0:32, r * 256 : r * 256 + 256] = v.reshape(8, 32, 256)

    head_of = lax.broadcasted_iota(jnp.int32, (128, 256), 0) // 32

    def step(new, new_scores, now, now_scores, now_max):
        new_max, total = [None, None], [None, None]
        if new is not None:
            h, first = new
            tile = h // 4
            q = [
                jnp.where(
                    head_of == h % 4, qt[first + u, tile * 128 : tile * 128 + 128, :].astype(F32), 0.0
                ).astype(BF16)
                for u in range(2)
            ]
        for jc in range(4):
            rows = slice(jc * 256, jc * 256 + 256)
            if new is not None:
                b = bias[h, jc].reshape(256, 256)
                for u in range(2):
                    m = maskb[first + u, rows, :]
                    sc = jnp.dot(kt[first + u, tile, rows, :], q[u], preferred_element_type=F32)
                    sc = sc + b + jnp.concatenate([m, m], 1)
                    new_scores[u][rows, :] = sc
                    f = fold_max(sc)
                    new_max[u] = f if new_max[u] is None else jnp.maximum(new_max[u], f)
            if now is not None:
                hn, start = now
                for u in range(2):
                    e = jnp.exp2(now_scores[u][rows, :] - now_max[u]).astype(BF16)
                    a = jnp.dot(vt[start + u, hn, :, rows], e, preferred_element_type=F32)
                    total[u] = a if total[u] is None else total[u] + a
        if now is not None:
            for u in range(2):
                att[start + u, hn * 32 : hn * 32 + 32, :] = total[u][:32] / total[u][32:33]
        if new is not None:
            return tuple(jnp.max(m, axis=0, keepdims=True) for m in new_max)

    sets = ((s0, s1), (s2, s3))
    last = [None, None, 0]

    def attend_to(*items):
        for new in items:
            now, top, n = last
            number = n + 1
            scores = sets[number % 2]
            last[:] = new, step(new, scores, now, sets[n % 2], top), number

    second_forward(0)
    second(2)
    first(3)
    pass_on(0)
    share(2)
    pass_on(1)
    project_all(0)
    share(3)
    pass_on(2)
    project_all(1)
    second_forward(1)
    second(3)
    finish(0)
    pass_on(3)
    attend_to((0, 0), (0, 2), (1, 0), (1, 2))
    project_all(2)
    attend_to((0, 4), (1, 4))
    project_all(3)
    second_forward(2)
    attend_to((0, 6), (1, 6))
    finish(1)
    attend_to((2, 0), (2, 2), (2, 4), (2, 6))
    second_forward(3)
    attend_to((3, 0), (3, 2), (3, 4), (3, 6))
    for k in (2, 3):
        finish(k)
        attend_to(*((h, 2 * g) for h in (2 * k, 2 * k + 1) for g in range(4)))
    step(None, None, last[0], sets[last[2] % 2], last[1])

    for s in range(8):
        out_ref[s] = (jnp.transpose(att[s]) * gate[s]).astype(BF16)
    sender.wait_sent()


def transition_kernel(
    x_ref, gated_ref, pair_ref, mask_ref, res_ref, wo_ref, w1_ref, w2_ref, wlr_ref, ow_ref,
    align_ref, out_ref,
    lscr, rscr, raw, left, maskall, rsend, rrecv, rt, obuf, upd, counts, col_scr,
    send_sems, recv_sems, r_send_sems, r_recv_sems, pass_sems,
):
    p = Place()
    home = p.c // 8
    core_peer = p.at(core=1 - p.core)
    receives = lax.rem(home, 2) == p.core
    greeted = p.along_with_pair(True) + p.along_with_pair(False) + [core_peer]
    barrier = greet(greeted)

    @pl.loop(0, 32)
    def _(c):
        @pl.when(jnp.logical_and(receives, jnp.logical_or(home != p.r, c != p.c)))
        def _():
            pl.semaphore_signal(barrier, inc=1, device_id=(home, c), device_id_type=MESH)

    sender = Sender(send_sems, recv_sems)
    mask = mask_ref[...].astype(F32)

    wl_t = wlr_ref[0:32, :]
    wr = wlr_ref[32:64, :]
    wr4 = jnp.concatenate([wr, wr, wr, wr], 0)
    mask_cols = jnp.transpose(mask)

    def transition_block(t, q):
        half = slice(t * 128, t * 128 + 128)
        four = slice(4 * q, 4 * q + 4)
        rows = x_ref[four, half, :].reshape(512, 256).astype(F32)
        gated = gated_ref[four, half, :].reshape(512, 256)
        after = rows + jnp.dot(gated, wo_ref[...], preferred_element_type=F32)
        hidden = jnp.dot(layer_norm(after).astype(BF16), w1_ref[...], preferred_element_type=F32)
        hidden = jnp.maximum(hidden, 0.0).astype(BF16)
        after = after + jnp.dot(hidden, w2_ref[...], preferred_element_type=F32)
        align_ref[four, half, :] = after.astype(BF16).reshape(4, 128, 256)
        n = layer_norm(after).astype(BF16)
        l = lax.dot_general(wl_t, n, NT, preferred_element_type=F32)
        rr = lax.dot_general(n, wr4, NT, preferred_element_type=F32)
        for u in range(4):
            s = 4 * q + u
            cols = slice(u * 128, u * 128 + 128)
            lscr[t, s * 32 : s * 32 + 32, :] = l[:, cols] * mask[s : s + 1, half]
            start = s * 256 + t * 128
            rscr[start : start + 128, :] = rr[cols] * mask_cols[half, s : s + 1]

    def own_left(t, a):
        return lscr[t, pl.ds(a, 8, stride=32), :]

    def fill_left(t):
        for a in range(16):
            both = jnp.concatenate([own_left(t, a), own_left(t, a + 16)], 0)
            raw[t, p.x, p.y, p.zl, :, a * 128 : a * 128 + 128] = both.astype(BF16)

    def left_part(t, part):
        lanes = pl.ds(part * 1024, 1024)
        view = lambda x, y: raw.at[t, window(x), window(y), pl.ds(0, 2), pl.ds(0, 16), lanes]
        own = raw.at[t, p.x, p.y, p.zl, pl.ds(0, 16), lanes]
        return PlaneGather(p, sender, view, part == 0), own, p.along_with_pair(part == 0)

    def mask_view(x, y):
        return maskall.at[window(x), window(y), pl.ds(0, 2), pl.ds(0, 16)]

    mask_unit = (
        PlaneGather(p, sender, mask_view, False),
        maskall.at[p.x, p.y, p.zl, pl.ds(0, 16)],
        p.along_with_pair(False),
    )
    halves = [[left_part(0, 0), left_part(0, 1), mask_unit], [left_part(1, 0), left_part(1, 1)]]

    def first(t):
        for unit, own, devices in halves[t]:
            unit.first(own, devices)

    def second(t):
        for unit, _, _ in halves[t]:
            unit.second()

    def second_forward(t):
        for unit, _, _ in halves[t]:
            unit.second_forward()

    def finish(t):
        for unit, _, _ in halves[t]:
            unit.finish()

    lane = lax.broadcasted_iota(jnp.int32, (8, 128), 1) // 32

    def right_copy(k, zh):
        return pltpu.make_async_remote_copy(
            src_ref=rsend.at[k],
            dst_ref=rrecv.at[p.c],
            send_sem=r_send_sems.at[k * 2 + zh],
            recv_sem=r_recv_sems.at[p.c],
            device_id=(zh * 2 + p.core, p.r * 8 + k),
            device_id_type=MESH,
        )

    def is_remote(k, zh):
        return jnp.logical_or(p.c != p.r * 8 + k, p.zh != zh)

    def send_right(t):
        for k in range(4 * t, 4 * t + 4):
            rows = []
            for half in range(2):
                parts = []
                for q in range(4):
                    j = k * 32 + half * 16 + q * 4
                    v = [rscr[pl.ds(j + u, 8, stride=256), :] for u in range(4)]
                    parts.append(
                        jnp.where(lane == 0, v[0], jnp.where(lane == 1, v[1], jnp.where(lane == 2, v[2], v[3])))
                    )
                parts.append(mask[:, t * 128 : t * 128 + 128])
                rows.append(jnp.concatenate(parts, 1))
            rsend[k] = jnp.concatenate(rows, 0).astype(BF16)

        @pl.loop(0, 8)
        def _(n):
            k, zh = 4 * t + n // 2, lax.rem(n, 2)

            @pl.when(is_remote(k, zh))
            def _():
                right_copy(k, zh).start()

            @pl.when(jnp.logical_not(is_remote(k, zh)))
            def _():
                pltpu.make_async_copy(rsend.at[k], rrecv.at[p.c], r_recv_sems.at[p.c]).start()

    right_pass = pltpu.make_async_remote_copy(
        src_ref=rrecv,
        dst_ref=rrecv,
        send_sem=pass_sems.at[0],
        recv_sem=pass_sems.at[1],
        device_id=core_peer,
        device_id_type=MESH,
    )

    transition_block(0, 0)
    transition_block(0, 1)
    fill_left(0)
    maskall[p.x, p.y, p.zl] = jnp.concatenate([mask, mask], 0).astype(BF16)
    pl.semaphore_wait(barrier, len(greeted) + 16 - (home == p.r).astype(jnp.int32))
    first(0)
    send_right(0)
    transition_block(1, 0)
    transition_block(1, 1)
    fill_left(1)
    second(0)
    first(1)
    send_right(1)
    ow_t = jnp.transpose(ow_ref[...].astype(F32)).astype(BF16)
    second_forward(0)
    second(1)

    @pl.when(receives)
    def _():
        @pl.loop(0, 32)
        def _(c):
            pltpu.make_async_copy(rrecv.at[c], rrecv.at[c], r_recv_sems.at[c]).wait()

        right_pass.start()

    @pl.when(jnp.logical_not(receives))
    def _():
        right_pass.wait_recv()

    place_in_tile = pl.multiple_of(lax.rem(p.c, 4) * 32, 32)
    for half in range(2):
        rows = rrecv[:, :, :].astype(F32)[:, half * 8 : half * 8 + 8, :].reshape(256, 640)
        rt[half * 512 : half * 512 + 512, :] = jnp.transpose(rows[:, :512]).astype(BF16)
        if half == 0:
            col_scr[...] = jnp.transpose(rows[:, 512:])
    mask_j = col_scr[pl.ds(place_in_tile, 32), :].astype(BF16)
    res = res_ref[...].astype(F32)
    rowid = lax.broadcasted_iota(jnp.int32, (8, 128), 0)
    pick = lambda n: jnp.sum(jnp.where(rowid == n, res, 0.0), 0, keepdims=True)
    res_i = jnp.concatenate([pick(p.r * 2), pick(p.r * 2 + 1)], 1)
    res_j = jnp.transpose(jnp.broadcast_to(pick(p.c // 4), (128, 128)))
    col_scr[:, 0:128] = res_j
    res_j = col_scr[pl.ds(place_in_tile, 32), 0:128]

    for t in range(2):
        finish(t)
        if t == 0:
            mask_i = maskall[...].astype(F32)[:, :, :, :8, :].reshape(256, 256).astype(BF16)
            pair_count = jnp.dot(mask_j, mask_i, preferred_element_type=F32) + COUNT_OFFSET
            factor = jnp.concatenate([res_j, res_j], 1) * res_i / pair_count
            counts[0] = factor[:, :128]
            counts[1] = factor[:, 128:]

        @pl.loop(0, 16)
        def _(n):
            x, y = n // 4, lax.rem(n, 4)
            two = raw[t, x, y].astype(F32)
            rows = pl.ds(pl.multiple_of(n * 16, 16), 16)
            for part in range(2):
                both = two[:, part * 8 : part * 8 + 8, :].reshape(16, 2048)
                left[rows, part * 2048 : part * 2048 + 2048] = both.astype(BF16)

        @pl.loop(0, 2)
        def _(n):
            for u in range(8):
                pair = n * 8 + u
                lanes = pl.ds(pl.multiple_of(pair * 256, 256), 256)
                o = jnp.dot(rt[...], left[:, lanes], preferred_element_type=F32).astype(BF16)
                for v in range(2):
                    obuf[:, pair * 2 + v] = o[:, v * 128 : v * 128 + 128].reshape(32, 32, 128)

        if t == 0:
            second_forward(1)

        @pl.loop(0, 2)
        def _(n):
            for u in range(8):
                j = n * 16 + u * 2
                two = jnp.concatenate([obuf[j + v].reshape(1024, 128) for v in range(2)], 1)
                o = jnp.dot(ow_t, two, preferred_element_type=F32)
                for v in range(2):
                    scale = counts[t, pl.ds(j + v, 1), :]
                    upd[pl.ds(t * 4096 + j + v, 128, stride=32), :] = jnp.transpose(o[:, v * 128 : v * 128 + 128] * scale)

        @pl.loop(0, 4)
        def _(n):
            rows = pl.ds(pl.multiple_of(t * 4096 + n * 1024, 1024), 1024)
            out_ref[rows, :] = (pair_ref[rows, :].astype(F32) + upd[rows, :]).astype(BF16)

    sender.wait_sent()

    @pl.when(receives)
    def _():
        right_pass.wait_send()

    @pl.loop(0, 16)
    def _(n):
        k, zh = n // 2, lax.rem(n, 2)

        @pl.when(is_remote(k, zh))
        def _():
            right_copy(k, zh).wait_send()


def vmem(n):
    return [pl.BlockSpec(memory_space=pltpu.VMEM)] * n


def attend(x, pair, mask, w, bw):
    copies = 8 + 3 + 12 + 8 * 7
    return pl.pallas_call(
        attention_kernel,
        out_shape=jax.ShapeDtypeStruct((8, 256, 256), BF16),
        in_specs=vmem(5),
        out_specs=pl.BlockSpec(memory_space=pltpu.VMEM),
        scratch_shapes=[
            pltpu.VMEM((8192, 128), F32),
            pltpu.VMEM((2, 256, 128), F32),
            pltpu.VMEM((8, 4, 4, 64, 256), F32),
            pltpu.VMEM((8, 4, 256, 256), BF16),
            pltpu.VMEM((4, 8, 256), F32),
            pltpu.VMEM((8, 1024, 128), F32),
            pltpu.VMEM((8, 2, 1024, 128), BF16),
            pltpu.VMEM((8, 8, 48, 1024), BF16),
            pltpu.VMEM((8, 256, 256), BF16),
            pltpu.VMEM((8, 256, 256), F32),
            pltpu.VMEM((8, 256, 256), F32),
        ]
        + [pltpu.VMEM((1024, 256), F32)] * 4
        + [pltpu.SemaphoreType.DMA((copies,)), pltpu.SemaphoreType.DMA((copies,))],
        compiler_params=pltpu.CompilerParams(collective_id=0, has_side_effects=True, vmem_limit_bytes=VMEM_BYTES),
    )(x, pair, mask, w, bw)


def transition(x, gated, pair, mask, res, wo, w1, w2, wlr, ow):
    copies = 5 * 11
    return pl.pallas_call(
        transition_kernel,
        out_shape=(
            jax.ShapeDtypeStruct((8, 256, 256), BF16),
            jax.ShapeDtypeStruct((8192, 128), BF16),
        ),
        in_specs=vmem(10),
        out_specs=tuple(vmem(2)),
        scratch_shapes=[
            pltpu.VMEM((2, 256, 128), F32),
            pltpu.VMEM((2048, 128), F32),
            pltpu.VMEM((2, 4, 4, 2, 16, 2048), BF16),
            pltpu.VMEM((256, 4096), BF16),
            pltpu.VMEM((4, 4, 2, 16, 256), BF16),
            pltpu.VMEM((8, 16, 640), BF16),
            pltpu.VMEM((32, 16, 640), BF16),
            pltpu.VMEM((1024, 256), BF16),
            pltpu.VMEM((32, 32, 32, 128), BF16),
            pltpu.VMEM((8192, 128), F32),
            pltpu.VMEM((2, 32, 128), F32),
            pltpu.VMEM((128, 256), F32),
            pltpu.SemaphoreType.DMA((copies,)),
            pltpu.SemaphoreType.DMA((copies,)),
            pltpu.SemaphoreType.DMA((16,)),
            pltpu.SemaphoreType.DMA((32,)),
            pltpu.SemaphoreType.DMA((2,)),
        ],
        compiler_params=pltpu.CompilerParams(collective_id=1, has_side_effects=True, vmem_limit_bytes=VMEM_BYTES),
    )(x, gated, pair, mask, res, wo, w1, w2, wlr, ow)


def per_device(x, pairwise, mask, residue_mask, w, wo, bw, w1, w2, wlr, ow):
    pair = pairwise.reshape(8192, 128)
    gated = attend(x, pair, mask, w, bw.T)
    alignment, new_pair = transition(x, gated, pair, mask, residue_mask.reshape(8, 128), wo, w1, w2, wlr.T, ow)
    return alignment, new_pair.reshape(256, 32, 128)


def solution(mesh):
    return jax.shard_map(
        per_device,
        mesh=mesh,
        in_specs=(P("col", "row", None), P("row", "col", None), P("col", "row")) + (P(),) * 8,
        out_specs=(P("col", "row", None), P("row", "col", None)),
        check_vma=False,
    )
```
